256 devices in a mesh: row: 32 (over y, x, core), col: 8 (over z).
Axes of the slice: x: 4, y: 4, z: 8, core: 2. Of those that a mesh axis runs over, the one named last changes fastest.
Arguments:
- tokens: bfloat16 [8192, 12288], P('row', 'col'), may hold values from -6 to 6
- weight_blocks: bfloat16 [96, 16, 128, 128], P('row', 'col'), may hold values from -0.1875 to 0.1875
- block_cols: int32 [96, 16], P(None, 'col'), may hold values from 0 to 23, as said below
- cotangent: bfloat16 [8192, 24576], P('row', 'col'), may hold values from -6 to 6
Outputs:
- activated: bfloat16 [8192, 24576], P('row', 'col')
- grad_tokens: bfloat16 [8192, 12288], P('row', 'col')
- grad_blocks: bfloat16 [96, 16, 128, 128], P('row', 'col')
The draws below stay inside these ranges and needn't reach their ends.
Inputs may be any that keep to these rules, and one draw needn't show every extreme that they name: `block_cols`: within each block row and panel the 2 entries are different block columns; the first entry of panel p in block row k is (k + o_p) mod 24 for an offset o_p of the panel.
All inputs are finite; a program needn't handle non-finite values.
Results may differ from the reference program's by a relative error of at most 0.022.
Values may be sent and summed in bfloat16 or wider, within the bound.
A program may use at most 128 MiB of HBM per device.

```python
import jax
import jax.numpy as jnp
from jax import lax

BLK = 128
D = 12288
NPANEL = 8
PB = 24
KP = 2
TOKENS = 8192
DB = 96
FF = 24576
N_ROW = 32
N_COL = 8


def draw_block_cols(key, part):
    key = jax.random.fold_in(key, 11)
    first_key, second_key = jax.random.split(key)
    offsets = jax.random.randint(first_key, (NPANEL,), 0, PB)
    diagonal = (jnp.arange(DB, dtype=jnp.int32)[:, None] + offsets[None, :]) % PB
    stride = jax.random.randint(second_key, (DB, NPANEL), 1, PB)
    partner = (diagonal + stride) % PB
    return jnp.stack([diagonal, partner], axis=2).reshape(DB, NPANEL * KP).astype(jnp.int32)


def spiked(result, rng, source, target, blocks, factor):
    def block_of(axis_at):
        return (jnp.arange(result.shape[axis_at]) // (result.shape[axis_at] // blocks)).reshape((-1,) + (1,) * (result.ndim - 1 - axis_at))

    first = jax.random.permutation(rng, blocks)[block_of(target)]
    far = (block_of(target) + blocks // 2) % blocks
    return jnp.where((block_of(source) == first) | (block_of(source) == far), factor * result, result)


def block_levels(stream_key, shape, cuts, least, largest):
    gain = 1.0
    for dim, blocks in cuts:
        steps = jax.random.uniform(jax.random.fold_in(jax.random.fold_in(stream_key, 6), dim), (blocks,), jnp.float32, least / len(cuts), largest / len(cuts))
        gain = gain * jnp.repeat(jnp.exp(steps), shape[dim] // blocks).reshape((-1,) + (1,) * (len(shape) - 1 - dim))
    return gain


def scatter_about(stream_key, dims, width, most, cuts=(), kind=jnp.bfloat16):
    loudness = block_levels(stream_key, dims, cuts, -0.22, 0.18) if cuts else 1.0
    values = jax.random.normal(stream_key, dims, jnp.float32) * width * loudness
    return jnp.minimum(jnp.maximum(values, -most), most).astype(kind)


def gaussian_with(stream_key, dims, width, most, pieces, heavy, kind=jnp.bfloat16):
    entries = width * jax.random.normal(stream_key, dims, jnp.float32)
    if pieces:
        entries = entries * block_levels(stream_key, dims, pieces, -0.22, 0.18)
    return jnp.clip(spiked(entries, jax.random.fold_in(stream_key, 3), *heavy), -most, most).astype(kind)


def setup_inputs(seed: int = 0) -> dict:
    splits = jax.random.split(jax.random.key(seed), 5)
    return {
        "tokens": gaussian_with(splits[0], (TOKENS, D), 1.0, 6.0, ((0, 32), (1, 8)), (0, 1, 32, 2.75)),
        "weight_blocks": scatter_about(splits[1], (DB, NPANEL * KP, BLK, BLK), (D * KP // PB) ** -0.5, 0.1875, ((0, 32), (1, 8))),
        "block_cols": draw_block_cols(jax.random.fold_in(splits[4], 71), 0),
        "cotangent": scatter_about(splits[3], (TOKENS, FF), 1.0, 6.0, ((0, 32), (1, 8))),
    }


def activate(values):
    return jax.nn.gelu(values, approximate=True)

def reference(tokens, weight_blocks, block_cols, cotangent):
    panel_group = NPANEL // N_COL
    token_blocks = tokens.astype(jnp.float32).reshape(TOKENS, DB, BLK)
    token_groups = token_blocks.reshape(N_ROW, TOKENS // N_ROW, DB, BLK)
    blocks_all = weight_blocks.reshape(DB, NPANEL, KP, BLK, BLK)
    cols_all = block_cols.reshape(DB, NPANEL, KP)
    cot_all = cotangent.reshape(TOKENS, NPANEL, PB * BLK)
    column_ids = jnp.arange(PB, dtype=jnp.int32)

    def panel_step(carry, panel_index):
        summed, group_sum = carry
        panel_weight = lax.dynamic_index_in_dim(blocks_all, panel_index, 1, keepdims=False).astype(jnp.float32)
        panel_cols = lax.dynamic_index_in_dim(cols_all, panel_index, 1, keepdims=False)
        onehot = (panel_cols[:, :, None] == column_ids[None, None, :]).astype(jnp.float32)
        products = jnp.einsum('tkd,ksdf->tksf', token_blocks, panel_weight)
        preact = jnp.einsum('tksf,ksj->tjf', products, onehot, precision=lax.Precision.HIGHEST).reshape(TOKENS, PB * BLK)
        act_value, pullback = jax.vjp(activate, preact)
        panel_cot = lax.dynamic_index_in_dim(cot_all, panel_index, 1, keepdims=False).astype(jnp.float32)
        grad_pre = pullback(panel_cot)[0].astype(jnp.bfloat16)
        grad_cols = grad_pre.astype(jnp.float32).reshape(TOKENS, PB, BLK)
        picked = jnp.einsum('tjf,ksj->tksf', grad_cols, onehot, precision=lax.Precision.HIGHEST)
        partial_value = jnp.einsum('tksf,ksdf->tkd', picked, panel_weight).reshape(TOKENS, D)
        group_sum = group_sum + partial_value
        closing = panel_index % panel_group == panel_group - 1
        rounded = lax.optimization_barrier(group_sum.astype(jnp.bfloat16)).astype(jnp.float32)
        summed = jnp.where(closing, summed + rounded, summed)
        group_sum = jnp.where(closing, jnp.zeros_like(group_sum), group_sum)
        picked_groups = picked.reshape(N_ROW, TOKENS // N_ROW, DB, KP, BLK)
        grad_parts = jnp.einsum('gtkd,gtksf->gksdf', token_groups, picked_groups)
        grad_parts = lax.optimization_barrier(grad_parts.astype(jnp.bfloat16)).astype(jnp.float32)
        grad_panel = lax.optimization_barrier(jnp.sum(grad_parts, axis=0)).astype(jnp.bfloat16)
        return ((summed, group_sum), (act_value.astype(jnp.bfloat16), grad_panel))
    start_sum = jnp.zeros((TOKENS, D), jnp.float32)
    (summed, group_sum), (acts, grads) = lax.scan(panel_step, (start_sum, start_sum), jnp.arange(NPANEL, dtype=jnp.int32))
    activated = jnp.transpose(acts, (1, 0, 2)).reshape(TOKENS, FF)
    grad_blocks = jnp.transpose(grads, (1, 0, 2, 3, 4)).reshape(DB, NPANEL * KP, BLK, BLK)
    grad_tokens = summed.astype(jnp.bfloat16)
    return (activated, grad_tokens, grad_blocks)
```

```python
import jax
import jax.numpy as jnp
from jax import lax
from jax.experimental import pallas as pl
from jax.experimental.pallas import tpu as pltpu
from jax.sharding import PartitionSpec as P

MESH = pl.DeviceIdType.MESH
F32 = jnp.float32
BF16 = jnp.bfloat16

BLK = 128
PB = 24
KP = 2
DB = 96
NX = 4
NZ = 8
ENT = DB * KP
PAIRS = (ENT + PB) // 2
CHUNKS = 2
T = 128
FEAT = 1536
FB = FEAT // BLK
NP = 2
PW = FEAT // NP
HALF = T // 2

AT_K = 0
AT_W = AT_K + 2 * PAIRS
AT_KEEP = AT_W + 2 * PAIRS
AT_LAST = AT_KEEP + PAIRS
AT_COL = AT_LAST + PB
AT_END = AT_COL + ENT


def weight_position(k):
    r, i = k // 3, k % 3
    core = r % 2
    x = (r // 2) % NX
    y = r // (2 * NX)
    a = x + (y - x) * core
    b = y + (x - y) * core
    return (((core * NX + a) * NX + b) * 3 + i) * 2


def plan(cols):
    c = cols.reshape(ENT)
    e = jnp.arange(ENT, dtype=jnp.int32)
    j = jnp.arange(PB, dtype=jnp.int32)
    hit = (c[:, None] == j[None, :]).astype(jnp.int32)
    count = jnp.sum(hit, axis=0)
    pairs = (count + 1) // 2
    base = jnp.sum(jnp.where(j[None, :] < j[:, None], pairs[None, :], 0), axis=1)
    rank = jnp.sum(((c[:, None] == c[None, :]) & (e[None, :] < e[:, None])).astype(jnp.int32), axis=1)
    at = jnp.sum(hit * (2 * base)[None, :], axis=1) + rank
    slot = jnp.arange(2 * PAIRS, dtype=jnp.int32)
    entry = jnp.sum(jnp.where(at[None, :] == slot[:, None], e[None, :] + 1, 0), axis=1) - 1
    row = jnp.maximum(entry, 0) // 2
    where = jnp.where(entry < 0, ENT, weight_position(row) + entry % 2)
    pair = jnp.arange(PAIRS, dtype=jnp.int32)
    keep = 1 - jnp.max((base[None, :] == pair[:, None]).astype(jnp.int32), axis=1)
    last = base + pairs - 1
    return jnp.concatenate([row, where, keep, last, c])


def kernel(
    idx, tok_hbm, w_hbm, cot_hbm,
    act_hbm, gt_hbm, gb_hbm,
    tok0, tok1, wg, seg, cot, act, gp0, gp1, dx0, dx1, rs0, rs1, dw, pr, bufa, bufb,
    load_sem, out_sem, ag_send_sem, ag_recv_sem, rs_send_sem, rs_recv_sem,
    wb_send, wb_recv, wa_send, wa_recv, wc_send, wc_recv,
    gc_send, gc_recv, ga_send, ga_recv, gb_send, gb_recv,
):
    toks, gps, dxs, rss = (tok0, tok1), (gp0, gp1), (dx0, dx1), (rs0, rs1)
    row, c = lax.axis_index("row"), lax.axis_index("col")
    core = row % 2
    x = (row // 2) % NX
    y = row // (2 * NX)
    a = x + (y - x) * core
    b = y + (x - y) * core

    def ring(v, step, n):
        return lax.rem(v + step + n, n)

    def chip(a_, b_):
        x_ = a_ + (b_ - a_) * core
        y_ = b_ + (a_ - b_) * core
        return ((y_ * NX + x_) * 2 + core, c)

    z_to = ((row, ring(c, 1, NZ)), (row, ring(c, -1, NZ)))
    a_to = (chip(ring(a, 1, NX), b), chip(ring(a, -1, NX), b))
    b_to = (chip(a, ring(b, 1, NX)), chip(a, ring(b, -1, NX)))
    sibling = (row + 1 - 2 * core, c)

    started = []

    def remote(src, dst, send, recv, to):
        return pltpu.make_async_remote_copy(
            src_ref=src, dst_ref=dst, send_sem=send, recv_sem=recv, device_id=to, device_id_type=MESH
        )

    def send(src, dst, send_sem, recv_sem, to):
        copy = remote(src, dst, send_sem, recv_sem, to)
        copy.start()
        started.append(copy)

    w_load = pltpu.make_async_copy(w_hbm, wg.at[pl.ds(((core * NX + a) * NX + b) * 6, 6)], load_sem.at[2])
    cot_load = pltpu.make_async_copy(cot_hbm, cot, load_sem.at[3])

    def tok_load(h):
        for i in range(FB):
            pltpu.make_async_copy(
                tok_hbm.at[pl.ds(h * T, T), pl.ds(i * BLK, BLK)], toks[h].at[c * FB + i], load_sem.at[h]
            ).start()

    def tok_wait(h):
        region = toks[h].at[pl.ds(c * FB, FB)]
        pltpu.make_async_copy(region, region, load_sem.at[h]).wait()

    tok_load(0)
    w_load.start()
    tok_load(1)
    cot_load.start()

    barrier = pltpu.get_barrier_semaphore()
    for to in (*z_to, *a_to, *b_to, sibling):
        pl.semaphore_signal(barrier, inc=1, device_id=to, device_id_type=MESH)
    pl.semaphore_wait(barrier, 7)

    def ag_region(h, shard, way, step, p):
        rows = pl.ds(0, T) if step < 4 else pl.ds(way * HALF, HALF)
        return toks[h].at[pl.ds(shard * FB + p * (FB // NP), FB // NP), rows]

    def ag_send(h, way, step, p):
        shard = ring(c, (1 - step) if way == 0 else (step - 1), NZ)
        region = ag_region(h, shard, way, step, p)
        sem = (h, way, step - 1, p)
        send(region, region, ag_send_sem.at[sem], ag_recv_sem.at[sem], z_to[way])

    def ag_event(h, step, p):
        for way in range(2):
            shard = ring(c, -step if way == 0 else step, NZ)
            region = ag_region(h, shard, way, step, p)
            sem = (h, way, step - 1, p)
            remote(region, region, ag_send_sem.at[sem], ag_recv_sem.at[sem], z_to[way]).wait_recv()
            if step < 4:
                ag_send(h, way, step + 1, p)

    def ag_open(h):
        for p in range(NP):
            for way in range(2):
                ag_send(h, way, 1, p)

    def w_region(core_, a_, b_, lo=0, n=6):
        return wg.at[pl.ds(((core_ * NX + a_) * NX + b_) * 6 + lo, n)]

    def b_of(q):
        return ring(b, (0, 1, -1, 2)[q], NX)

    def w_to_a(q):
        region = w_region(core, a, b_of(q))
        for way in range(2):
            send(region, region, wa_send.at[way, 0, q], wa_recv.at[way, 0, q], a_to[way])

    def w_to_sibling(g, q):
        region = w_region(core, ring(a, (0, 1, -1, 2)[g], NX), b_of(q))
        send(region, region, wc_send.at[g, q], wc_recv.at[g, q], sibling)

    def w_open():
        region = w_region(core, a, b)
        for way in range(2):
            send(region, region, wb_send.at[way, 0], wb_recv.at[way, 0], b_to[way])
        w_to_a(0)
        w_to_sibling(0, 0)

    def w_wait(region, send_sem, recv_sem, to):
        remote(region, region, send_sem, recv_sem, to).wait_recv()

    def w_near_b():
        for way in range(2):
            q = 2 if way == 0 else 1
            w_wait(w_region(core, a, b_of(q)), wb_send.at[way, 0], wb_recv.at[way, 0], b_to[way])
            region = w_region(core, a, b_of(q), 3 * way, 3)
            send(region, region, wb_send.at[way, 1], wb_recv.at[way, 1], b_to[way])
            w_to_a(q)
            w_to_sibling(0, q)

    def w_far_b():
        for way in range(2):
            w_wait(w_region(core, a, b_of(3), 3 * way, 3), wb_send.at[way, 1], wb_recv.at[way, 1], b_to[way])
        w_to_a(3)
        w_to_sibling(0, 3)

    def w_near_a(q):
        for way in range(2):
            g = 2 if way == 0 else 1
            a_ = ring(a, -1 if way == 0 else 1, NX)
            w_wait(w_region(core, a_, b_of(q)), wa_send.at[way, 0, q], wa_recv.at[way, 0, q], a_to[way])
            region = w_region(core, a_, b_of(q), 3 * way, 3)
            send(region, region, wa_send.at[way, 1, q], wa_recv.at[way, 1, q], a_to[way])
            w_to_sibling(g, q)

    def w_far_a(q):
        a_ = ring(a, 2, NX)
        for way in range(2):
            w_wait(w_region(core, a_, b_of(q), 3 * way, 3), wa_send.at[way, 1, q], wa_recv.at[way, 1, q], a_to[way])
        w_to_sibling(3, q)

    def w_close():
        for g in range(4):
            for q in range(4):
                a_ = ring(b, (0, 1, -1, 2)[g], NX)
                b_ = ring(a, (0, 1, -1, 2)[q], NX)
                w_wait(w_region(1 - core, a_, b_), wc_send.at[g, q], wc_recv.at[g, q], sibling)

    def lanes(k):
        return pl.ds(pl.multiple_of(k * BLK, BLK), BLK)

    def fwd(h, lo, hi):
        tok = toks[h]

        def body(i, acc):
            xs = jnp.concatenate([tok[idx[AT_K + 2 * i + s]] for s in range(2)], axis=1)
            ws = jnp.concatenate([wg[idx[AT_W + 2 * i + s]] for s in range(2)], axis=0)
            acc = acc * idx[AT_KEEP + i].astype(F32) + jnp.dot(xs, ws, preferred_element_type=F32)
            seg[i] = acc
            return acc

        start = jnp.zeros((T, BLK), F32) if lo == 0 else seg[lo - 1]
        lax.fori_loop(lo, hi, body, start, unroll=3)

    def gelu(h):
        rows = pl.ds(h * T, T)

        def body(j, carry):
            v = seg[idx[AT_LAST + j]]
            k0 = 0.7978845608028654
            v2 = v * v
            th = jnp.tanh(k0 * (v + 0.044715 * (v2 * v)))
            half = 0.5 * (1.0 + th)
            slope = half + (0.5 * v) * (1.0 - th * th) * (k0 * (1.0 + 3 * 0.044715 * v2))
            act[rows, lanes(j)] = (v * half).astype(BF16)
            gps[h][j] = (cot[rows, lanes(j)].astype(F32) * slope).astype(BF16)
            return carry

        lax.fori_loop(0, PB, body, 0)
        pltpu.make_async_copy(act.at[rows], act_hbm.at[rows], out_sem.at[h]).start()

    def grad_x(h, shard):
        gp, dx = gps[h], dxs[h]

        def body(i, carry):
            k = shard * (FB) + i
            at = weight_position(k)
            gs = jnp.concatenate([gp[idx[AT_COL + 2 * k + s]] for s in range(2)], axis=1)
            ws = jnp.concatenate([wg[at + s] for s in range(2)], axis=1)
            out = lax.dot_general(gs, ws, (((1,), (1,)), ((), ())), preferred_element_type=F32)
            dx[:, lanes(k)] = out.astype(BF16)
            return carry

        lax.fori_loop(0, FB, body, 0, unroll=3)

    def grad_w(core_, a_):
        def body(i, carry):
            b_, j = i // 3, i % 3
            at = (((core_ * NX + a_) * NX + b_) * 3 + j) * 2
            x_ = a_ + (b_ - a_) * core_
            y_ = b_ + (a_ - b_) * core_
            k = ((y_ * NX + x_) * 2 + core_) * 3 + j
            xs = jnp.concatenate([tok[k] for tok in toks], axis=0)
            cols = [idx[AT_COL + 2 * k + s] for s in range(2)]
            gs = jnp.concatenate(
                [jnp.concatenate([gp[col] for gp in gps], axis=0) for col in cols], axis=1
            )
            out = lax.dot_general(xs, gs, (((0,), (0,)), ((), ())), preferred_element_type=F32)
            dw[at] = out[:, :BLK].astype(BF16)
            dw[at + 1] = out[:, BLK:].astype(BF16)
            return carry

        lax.fori_loop(0, 12, body, 0, unroll=2)

    def rs_rows(way, step):
        return pl.ds(0, HALF) if step == 1 else pl.ds(HALF + (step - 2) * T, T)

    def rs_send(h, way, step, p):
        shard = ring(c, (5 - step) if way == 0 else (step - 5), NZ)
        col = pl.ds(pl.multiple_of(shard * FEAT + p * PW, PW), PW)
        rows = pl.ds(way * HALF, HALF) if step == 1 else pl.ds(0, T)
        sem = (h, way, step - 1, p)
        send(
            dxs[h].at[rows, col],
            rss[h].at[way, rs_rows(way, step), pl.ds(p * PW, PW)],
            rs_send_sem.at[sem],
            rs_recv_sem.at[sem],
            z_to[way],
        )

    def rs_open(h):
        for p in range(NP):
            for way in range(2):
                rs_send(h, way, 1, p)

    def rs_wait(h, way, step, p):
        region = rss[h].at[way, rs_rows(way, step), pl.ds(p * PW, PW)]
        sem = (h, way, step - 1, p)
        remote(region, region, rs_send_sem.at[sem], rs_recv_sem.at[sem], z_to[way]).wait_recv()

    def rs_event(h, step, p):
        dx, rs = dxs[h], rss[h]
        if step < 4:
            for way in range(2):
                rs_wait(h, way, step, p)
                shard = ring(c, (4 - step) if way == 0 else (step - 4), NZ)
                rows = pl.ds(way * HALF, HALF) if step == 1 else pl.ds(0, T)

                def body(i, carry):
                    at = lanes(shard * (FB) + p * (PW // BLK) + i)
                    got = rs[way, rs_rows(way, step), lanes(p * (PW // BLK) + i)]
                    dx[rows, at] = (dx[rows, at].astype(F32) + got.astype(F32)).astype(BF16)
                    return carry

                lax.fori_loop(0, PW // BLK, body, 0, unroll=2)
                rs_send(h, way, step + 1, p)
        else:
            for way in range(2):
                rs_wait(h, way, step, p)

            def body(i, carry):
                at = lanes(c * (FB) + p * (PW // BLK) + i)
                total = dx[:, at].astype(F32)
                for way in range(2):
                    total += rs[way, rs_rows(way, 4), lanes(p * (PW // BLK) + i)].astype(F32)
                dx[:, at] = total.astype(BF16)
                return carry

            lax.fori_loop(0, PW // BLK, body, 0, unroll=2)
            pltpu.make_async_copy(
                dx.at[:, pl.ds(pl.multiple_of(c * FEAT + p * PW, PW), PW)],
                gt_hbm.at[pl.ds(h * T, T), pl.ds(p * PW, PW)],
                out_sem.at[2 + h * NP + p],
            ).start()

    def w_at(a_, b_=0):
        return ((core * NX + a_) * NX + b_) * 6

    def pair_send(a_):
        src = dw.at[pl.ds((((1 - core) * NX + a_) * NX) * 6, 24)]
        send(src, pr.at[pl.ds(a_ * 24, 24)], gc_send.at[a_], gc_recv.at[a_], sibling)

    def add_blocks(dst, n, *srcs):
        def body(i, carry):
            total = dw[dst + i].astype(F32)
            for ref, at in srcs:
                total += ref[at + i].astype(F32)
            dw[dst + i] = total.astype(BF16)
            return carry

        lax.fori_loop(0, n, body, 0, unroll=2)

    def pair_add(a_):
        region = pr.at[pl.ds(a_ * 24, 24)]
        remote(region, region, gc_send.at[a_], gc_recv.at[a_], sibling).wait_recv()
        add_blocks(w_at(a_), 24, (pr, a_ * 24))

    def hop(buf, way, step, size, src, sems, to):
        off = way * (size + size // 2) + (0 if step == 0 else size // 2)
        n = size // 2 if step == 0 else size
        dst = buf.at[pl.ds(off, n)]
        return remote(dw.at[pl.ds(src, n)], dst, sems[0].at[way, step], sems[1].at[way, step], to), off

    def ring_open(buf, far, size, sems, tos):
        for way in range(2):
            copy, _ = hop(buf, way, 0, size, far + way * (size // 2), sems, tos[way])
            copy.start()
            started.append(copy)

    def ring_middle(buf, nexts, size, sems, tos):
        for way in range(2):
            copy, off = hop(buf, way, 0, size, 0, sems, tos[way])
            copy.wait_recv()
            add_blocks(nexts[way] + way * (size // 2), size // 2, (buf, off))
            copy, _ = hop(buf, way, 1, size, nexts[way], sems, tos[way])
            copy.start()
            started.append(copy)

    def ring_close(buf, own, size, sems, tos):
        srcs = []
        for way in range(2):
            copy, off = hop(buf, way, 1, size, 0, sems, tos[way])
            copy.wait_recv()
            srcs.append((buf, off))
        add_blocks(own, size, *srcs)

    a_sems, b_sems = (ga_send, ga_recv), (gb_send, gb_recv)
    a_near = (w_at(ring(a, 1, NX)), w_at(ring(a, -1, NX)))
    b_near = (w_at(a, ring(b, 1, NX)), w_at(a, ring(b, -1, NX)))

    wg[ENT] = jnp.zeros((BLK, BLK), BF16)
    tok_wait(0)
    ag_open(0)
    w_load.wait()
    w_open()
    w_near_b()
    w_near_a(0)
    w_far_b()
    ag_event(0, 1, 0)
    w_near_a(1)
    w_near_a(2)
    ag_event(0, 1, 1)
    w_near_a(3)
    w_far_a(0)
    w_far_a(1)
    w_far_a(2)
    ag_event(0, 2, 0)
    w_far_a(3)
    ag_event(0, 2, 1)
    ag_event(0, 3, 0)
    tok_wait(1)
    ag_event(0, 3, 1)
    ag_open(1)
    cot_load.wait()
    w_close()
    ag_event(0, 4, 0)
    ag_event(0, 4, 1)

    quarter = PAIRS // 4
    fwd(0, 0, quarter)
    ag_event(1, 1, 0)
    fwd(0, quarter, 2 * quarter)
    ag_event(1, 1, 1)
    fwd(0, 2 * quarter, 3 * quarter)
    fwd(0, 3 * quarter, PAIRS)
    ag_event(1, 2, 0)
    gelu(0)
    grad_x(0, ring(c, 4, NZ))
    ag_event(1, 2, 1)
    grad_x(0, ring(c, 3, NZ))
    grad_x(0, ring(c, -3, NZ))
    grad_x(0, ring(c, 2, NZ))
    ag_event(1, 3, 0)
    grad_x(0, ring(c, -2, NZ))
    grad_x(0, ring(c, 1, NZ))
    grad_x(0, ring(c, -1, NZ))
    grad_x(0, c)
    ag_event(1, 3, 1)
    rs_open(0)
    ag_event(1, 4, 0)
    ag_event(1, 4, 1)

    fwd(1, 0, quarter)
    rs_event(0, 1, 0)
    rs_event(0, 1, 1)
    fwd(1, quarter, 2 * quarter)
    fwd(1, 2 * quarter, 3 * quarter)
    rs_event(0, 2, 0)
    fwd(1, 3 * quarter, PAIRS)
    rs_event(0, 2, 1)
    gelu(1)
    grad_x(1, ring(c, 4, NZ))
    rs_open(1)
    grad_x(1, ring(c, 3, NZ))
    grad_x(1, ring(c, -3, NZ))
    rs_event(0, 3, 0)
    grad_x(1, ring(c, 2, NZ))
    grad_x(1, ring(c, -2, NZ))
    rs_event(0, 3, 1)
    rs_event(1, 1, 0)
    grad_x(1, ring(c, 1, NZ))
    grad_x(1, ring(c, -1, NZ))
    rs_event(1, 1, 1)
    grad_x(1, c)
    for g in range(2):
        grad_w(1 - core, g)
        pair_send(g)
    rs_event(0, 4, 0)
    for g in range(2, 4):
        grad_w(1 - core, g)
        pair_send(g)
    rs_event(0, 4, 1)
    rs_event(1, 2, 0)
    grad_w(core, ring(a, 2, NX))
    grad_w(core, ring(a, 1, NX))
    pair_add(ring(a, 2, NX))
    ring_open(bufa, w_at(ring(a, 2, NX)), 24, a_sems, a_to)
    rs_event(1, 2, 1)
    grad_w(core, ring(a, -1, NX))
    grad_w(core, a)
    pair_add(ring(a, 1, NX))
    pair_add(ring(a, -1, NX))
    pair_add(a)
    ring_middle(bufa, a_near, 24, a_sems, a_to)
    rs_event(1, 3, 0)
    ring_close(bufa, w_at(a), 24, a_sems, a_to)
    ring_open(bufb, w_at(a, ring(b, 2, NX)), 6, b_sems, b_to)
    rs_event(1, 3, 1)
    ring_middle(bufb, b_near, 6, b_sems, b_to)
    ring_close(bufb, w_at(a, b), 6, b_sems, b_to)
    last = pltpu.make_async_copy(dw.at[pl.ds(w_at(a, b), 6)], gb_hbm, out_sem.at[2 + CHUNKS * NP])
    last.start()
    rs_event(1, 4, 0)
    rs_event(1, 4, 1)

    last.wait()
    for h in range(CHUNKS):
        rows = pl.ds(h * T, T)
        pltpu.make_async_copy(act.at[rows], act_hbm.at[rows], out_sem.at[h]).wait()
        for p in range(NP):
            pltpu.make_async_copy(
                dxs[h].at[:, pl.ds(pl.multiple_of(c * FEAT + p * PW, PW), PW)],
                gt_hbm.at[pl.ds(h * T, T), pl.ds(p * PW, PW)],
                out_sem.at[2 + h * NP + p],
            ).wait()
    for copy in started:
        copy.wait_send()


def on_device(tokens, weight_blocks, block_cols, cotangent):
    idx = plan(block_cols)
    any_space = pl.BlockSpec(memory_space=pl.ANY)
    dma = pltpu.SemaphoreType.DMA
    act, grad_tokens, grad_blocks = pl.pallas_call(
        kernel,
        out_shape=(
            jax.ShapeDtypeStruct((CHUNKS * T, PB * BLK), BF16),
            jax.ShapeDtypeStruct((CHUNKS * T, FEAT), BF16),
            jax.ShapeDtypeStruct((6, BLK, BLK), BF16),
        ),
        in_specs=[pl.BlockSpec(memory_space=pltpu.SMEM), any_space, any_space, any_space],
        out_specs=(any_space, any_space, any_space),
        scratch_shapes=[
            pltpu.VMEM((DB, T, BLK), BF16),
            pltpu.VMEM((DB, T, BLK), BF16),
            pltpu.VMEM((ENT + 1, BLK, BLK), BF16),
            pltpu.VMEM((PAIRS, T, BLK), F32),
            pltpu.VMEM((CHUNKS * T, PB * BLK), BF16),
            pltpu.VMEM((CHUNKS * T, PB * BLK), BF16),
            pltpu.VMEM((PB, T, BLK), BF16),
            pltpu.VMEM((PB, T, BLK), BF16),
            pltpu.VMEM((T, DB * BLK), BF16),
            pltpu.VMEM((T, DB * BLK), BF16),
            pltpu.VMEM((2, HALF + 3 * T, FEAT), BF16),
            pltpu.VMEM((2, HALF + 3 * T, FEAT), BF16),
            pltpu.VMEM((ENT, BLK, BLK), BF16),
            pltpu.VMEM((ENT // 2, BLK, BLK), BF16),
            pltpu.VMEM((2 * 36, BLK, BLK), BF16),
            pltpu.VMEM((2 * 9, BLK, BLK), BF16),
            dma((4,)),
            dma((2 + CHUNKS * NP + 1,)),
            dma((CHUNKS, 2, 4, NP)),
            dma((CHUNKS, 2, 4, NP)),
            dma((CHUNKS, 2, 4, NP)),
            dma((CHUNKS, 2, 4, NP)),
            dma((2, 2)),
            dma((2, 2)),
            dma((2, 2, 4)),
            dma((2, 2, 4)),
            dma((4, 4)),
            dma((4, 4)),
            dma((4,)),
            dma((4,)),
            dma((2, 2)),
            dma((2, 2)),
            dma((2, 2)),
            dma((2, 2)),
        ],
        compiler_params=pltpu.CompilerParams(
            collective_id=0, has_side_effects=True, vmem_limit_bytes=60 * 1024 * 1024
        ),
        cost_estimate=pl.CostEstimate(flops=4_831_838_208, bytes_accessed=6_000_000, transcendentals=786_432),
    )(idx, tokens, weight_blocks.reshape(6, BLK, BLK), cotangent)
    return act, grad_tokens, grad_blocks.reshape(3, KP, BLK, BLK)


def solution(mesh):
    return jax.shard_map(
        on_device,
        mesh=mesh,
        in_specs=(P("row", "col"), P("row", "col", None, None), P(None, "col"), P("row", "col")),
        out_specs=(P("row", "col"), P("row", "col"), P("row", "col", None, None)),
        check_vma=False,
    )
```

```python
import jax
import jax.numpy as jnp
from jax import lax
from jax.experimental import pallas as pl
from jax.experimental.pallas import tpu as pltpu
from jax.sharding import PartitionSpec as P

MESH = pl.DeviceIdType.MESH
F32 = jnp.float32
BF16 = jnp.bfloat16

BLK = 128
PB = 24
KP = 2
DB = 96
NX = 4
NZ = 8
ENT = DB * KP
PAIRS = (ENT + PB) // 2
CHUNKS = 2
T = 128
FEAT = 1536
FB = FEAT // BLK
NP = 2
PW = FEAT // NP
HALF = T // 2

TAB_K, TAB_KEEP, TAB_LAST, TAB_W = 0, 8, 16, 24


def weight_position(k):
    r, i = k // 3, k % 3
    core = r % 2
    x = (r // 2) % NX
    y = r // (2 * NX)
    a = x + (y - x) * core
    b = y + (x - y) * core
    return (((core * NX + a) * NX + b) * 3 + i) * 2


def kernel(
    cols_hbm, tok_hbm, w_hbm, cot_hbm,
    act_hbm, gt_hbm, gb_hbm,
    tok0, tok1, wg, seg, cot, act, gp0, gp1, dx0, dx1, rs0, rs1, dw, pr, bufa, bufb,
    cols_v, cols, count_v, count, place_v, place, tab_v, tab,
    load_sem, out_sem, send_sem, ag_sem, rs_sem, wb_sem, wa_sem, wc_sem, gc_sem, ga_sem, gb_sem,
):
    toks, gps, dxs, rss = (tok0, tok1), (gp0, gp1), (dx0, dx1), (rs0, rs1)
    row, c = lax.axis_index("row"), lax.axis_index("col")
    core = row % 2
    x = (row // 2) % NX
    y = row // (2 * NX)
    a = x + (y - x) * core
    b = y + (x - y) * core

    def ring(v, step, n):
        return lax.rem(v + step + n, n)

    def chip(a_, b_):
        x_ = a_ + (b_ - a_) * core
        y_ = b_ + (a_ - b_) * core
        return ((y_ * NX + x_) * 2 + core, c)

    z_to = ((row, ring(c, 1, NZ)), (row, ring(c, -1, NZ)))
    a_to = (chip(ring(a, 1, NX), b), chip(ring(a, -1, NX), b))
    b_to = (chip(a, ring(b, 1, NX)), chip(a, ring(b, -1, NX)))
    sibling = (row + 1 - 2 * core, c)

    def remote(src, dst, sends, recv, to):
        return pltpu.make_async_remote_copy(
            src_ref=src, dst_ref=dst, send_sem=send_sem.at[sends], recv_sem=recv, device_id=to, device_id_type=MESH
        )

    def send(src, dst, sends, recv, to):
        remote(src, dst, sends, recv, to).start()

    def landed(region, recv):
        pltpu.make_async_copy(region, region, recv).wait()

    def out(src, dst, at):
        pltpu.make_async_copy(src, dst, out_sem.at[at]).start()

    w_load = pltpu.make_async_copy(w_hbm, wg.at[pl.ds(((core * NX + a) * NX + b) * 6, 6)], load_sem.at[2])
    cot_load = pltpu.make_async_copy(cot_hbm, cot, load_sem.at[3])

    def tok_load(h):
        for i in range(FB):
            pltpu.make_async_copy(
                tok_hbm.at[pl.ds(h * T, T), pl.ds(i * BLK, BLK)], toks[h].at[c * FB + i], load_sem.at[h]
            ).start()

    def tok_wait(h):
        region = toks[h].at[pl.ds(c * FB, FB)]
        pltpu.make_async_copy(region, region, load_sem.at[h]).wait()

    tok_load(0)
    w_load.start()
    pltpu.make_async_copy(cols_hbm, cols, load_sem.at[4]).start()
    pltpu.make_async_copy(cols_hbm, cols_v, load_sem.at[5]).start()
    tok_load(1)
    cot_load.start()

    barrier = pltpu.get_barrier_semaphore()
    for to in (*z_to, *a_to, *b_to, sibling):
        pl.semaphore_signal(barrier, inc=1, device_id=to, device_id_type=MESH)
    pl.semaphore_wait(barrier, 7)

    def ag_region(h, shard, way, step, p):
        rows = pl.ds(0, T) if step < 4 else pl.ds(way * HALF, HALF)
        return toks[h].at[pl.ds(shard * FB + p * (FB // NP), FB // NP), rows]

    def ag_at(way, step):
        return 6 if step == 4 else 2 * (step - 1) + way

    def ag_send(h, way, step, p):
        shard = ring(c, (1 - step) if way == 0 else (step - 1), NZ)
        region = ag_region(h, shard, way, step, p)
        send(region, region, h, ag_sem.at[h, ag_at(way, step), p], z_to[way])

    def ag_event(h, step, p):
        if step == 4:
            landed(ag_region(h, ring(c, 4, NZ), 0, 1, p), ag_sem.at[h, 6, p])
            return
        for way in range(2):
            shard = ring(c, -step if way == 0 else step, NZ)
            landed(ag_region(h, shard, way, step, p), ag_sem.at[h, ag_at(way, step), p])
            ag_send(h, way, step + 1, p)

    def ag_open(h):
        for p in range(NP):
            for way in range(2):
                ag_send(h, way, 1, p)

    def w_region(core_, a_, b_, lo=0, n=6):
        return wg.at[pl.ds(((core_ * NX + a_) * NX + b_) * 6 + lo, n)]

    def b_of(q):
        return ring(b, (0, 1, -1, 2)[q], NX)

    def w_to_a(q):
        region = w_region(core, a, b_of(q))
        for way in range(2):
            send(region, region, 4, wa_sem.at[way, q], a_to[way])

    def w_to_sibling(g, q):
        region = w_region(core, ring(a, (0, 1, -1, 2)[g], NX), b_of(q))
        send(region, region, 4, wc_sem.at[0], sibling)

    def w_open():
        region = w_region(core, a, b)
        for way in range(2):
            send(region, region, 4, wb_sem.at[way], b_to[way])
        w_to_a(0)
        w_to_sibling(0, 0)

    def w_near_b():
        for way in range(2):
            q = 2 if way == 0 else 1
            landed(w_region(core, a, b_of(q)), wb_sem.at[way])
            region = w_region(core, a, b_of(q), 3 * way, 3)
            send(region, region, 4, wb_sem.at[2], b_to[way])
            w_to_a(q)
            w_to_sibling(0, q)

    def w_far_b():
        landed(w_region(core, a, b_of(3)), wb_sem.at[2])
        w_to_a(3)
        w_to_sibling(0, 3)

    def w_near_a(q):
        for way in range(2):
            g = 2 if way == 0 else 1
            a_ = ring(a, -1 if way == 0 else 1, NX)
            landed(w_region(core, a_, b_of(q)), wa_sem.at[way, q])
            region = w_region(core, a_, b_of(q), 3 * way, 3)
            send(region, region, 4, wa_sem.at[2, q], a_to[way])
            w_to_sibling(g, q)

    def w_far_a(q):
        landed(w_region(core, ring(a, 2, NX), b_of(q)), wa_sem.at[2, q])
        w_to_sibling(3, q)

    def w_close():
        landed(wg.at[pl.ds((1 - core) * DB, DB)], wc_sem.at[0])

    def plan_places():
        pltpu.make_async_copy(cols_hbm, cols, load_sem.at[4]).wait()
        pltpu.make_async_copy(cols_hbm, cols_v, load_sem.at[5]).wait()
        mine = cols_v[...]
        order = lax.broadcasted_iota(jnp.int32, (KP, DB), 0) * DB + lax.broadcasted_iota(jnp.int32, (KP, DB), 1)
        lane = lax.broadcasted_iota(jnp.int32, (8, BLK), 1)

        def body(k, carry):
            at, counts = carry
            for s in range(KP):
                col = cols[s, k]
                before = (col < mine) | ((col == mine) & (s * DB + k < order))
                at = at + jnp.where(before, 1, 0)
                counts = counts + jnp.where(lane == col, 1, 0)
            return at, counts

        at, counts = lax.fori_loop(
            0, DB, body, (jnp.zeros((KP, DB), jnp.int32), jnp.zeros((8, BLK), jnp.int32)), unroll=4
        )
        count_v[...] = counts
        copy = pltpu.make_async_copy(count_v, count, load_sem.at[6])
        copy.start()
        copy.wait()
        pair = lane
        keep = jnp.ones((8, BLK), jnp.int32)
        last = jnp.full((8, BLK), -1, jnp.int32)
        base = jnp.int32(0)
        for j in range(PB):
            n = count[0, j]
            pairs = lax.shift_right_logical(n + 1, 1)
            at = at + jnp.where(mine > j, n & 1, 0)
            keep = jnp.where(pair == base, 0, keep)
            last = last + jnp.where(lane >= j, pairs, 0)
            base = base + pairs
        place_v[...] = at
        copy = pltpu.make_async_copy(place_v, place, load_sem.at[6])
        copy.start()
        copy.wait()
        tab_v[pl.ds(8, 8)] = keep
        tab_v[pl.ds(16, 8)] = last

    def plan_table():
        slot = 2 * lax.broadcasted_iota(jnp.int32, (8, BLK), 1) + lax.broadcasted_iota(jnp.int32, (8, BLK), 0)

        def body(k, carry):
            rows, where = carry
            first = weight_position(k)
            for s in range(KP):
                hit = slot == place[s, k]
                rows = jnp.where(hit, k, rows)
                where = jnp.where(hit, first + s, where)
            return rows, where

        rows, where = lax.fori_loop(
            0, DB, body, (jnp.zeros((8, BLK), jnp.int32), jnp.full((8, BLK), ENT, jnp.int32)), unroll=2
        )
        tab_v[pl.ds(0, 8)] = rows
        tab_v[pl.ds(24, 8)] = where
        copy = pltpu.make_async_copy(tab_v, tab, load_sem.at[6])
        copy.start()
        copy.wait()

    def lanes(k):
        return pl.ds(pl.multiple_of(k * BLK, BLK), BLK)

    def fwd(h, lo, hi):
        tok = toks[h]

        def body(i, acc):
            xs = jnp.concatenate([tok[tab[TAB_K + s, i]] for s in range(2)], axis=1)
            ws = jnp.concatenate([wg[tab[TAB_W + s, i]] for s in range(2)], axis=0)
            acc = acc * tab[TAB_KEEP, i].astype(F32) + jnp.dot(xs, ws, preferred_element_type=F32)
            seg[i] = acc
            return acc

        start = jnp.zeros((T, BLK), F32) if lo == 0 else seg[lo - 1]
        lax.fori_loop(lo, hi, body, start, unroll=3)

    def gelu(h):
        rows = pl.ds(h * T, T)

        def body(j, carry):
            v = seg[tab[TAB_LAST, j]]
            k0 = 0.7978845608028654
            v2 = v * v
            th = jnp.tanh(k0 * (v + 0.044715 * (v2 * v)))
            half = 0.5 * (1.0 + th)
            slope = half + (0.5 * v) * (1.0 - th * th) * (k0 * (1.0 + 3 * 0.044715 * v2))
            act[rows, lanes(j)] = (v * half).astype(BF16)
            gps[h][j] = (cot[rows, lanes(j)].astype(F32) * slope).astype(BF16)
            return carry

        lax.fori_loop(0, PB, body, 0)
        out(act.at[rows], act_hbm.at[rows], 0)

    def grad_x(h, shard):
        gp, dx = gps[h], dxs[h]

        def body(i, carry):
            k = shard * FB + i
            at = weight_position(k)
            gs = jnp.concatenate([gp[cols[s, k]] for s in range(2)], axis=1)
            ws = jnp.concatenate([wg[at + s] for s in range(2)], axis=1)
            out = lax.dot_general(gs, ws, (((1,), (1,)), ((), ())), preferred_element_type=F32)
            dx[:, lanes(k)] = out.astype(BF16)
            return carry

        lax.fori_loop(0, FB, body, 0, unroll=3)

    def grad_w(core_, a_):
        def body(i, carry):
            b_, j = i // 3, i % 3
            at = (((core_ * NX + a_) * NX + b_) * 3 + j) * 2
            x_ = a_ + (b_ - a_) * core_
            y_ = b_ + (a_ - b_) * core_
            k = ((y_ * NX + x_) * 2 + core_) * 3 + j
            xs = jnp.concatenate([tok[k] for tok in toks], axis=0)
            picks = [cols[s, k] for s in range(2)]
            gs = jnp.concatenate(
                [jnp.concatenate([gp[col] for gp in gps], axis=0) for col in picks], axis=1
            )
            out = lax.dot_general(xs, gs, (((0,), (0,)), ((), ())), preferred_element_type=F32)
            dw[at] = out[:, :BLK].astype(BF16)
            dw[at + 1] = out[:, BLK:].astype(BF16)
            return carry

        lax.fori_loop(0, 12, body, 0, unroll=2)

    def rs_rows(way, step):
        return pl.ds(0, HALF) if step == 1 else pl.ds(HALF + (step - 2) * T, T)

    def rs_send(h, way, step, p):
        shard = ring(c, (5 - step) if way == 0 else (step - 5), NZ)
        col = pl.ds(pl.multiple_of(shard * FEAT + p * PW, PW), PW)
        rows = pl.ds(way * HALF, HALF) if step == 1 else pl.ds(0, T)
        send(
            dxs[h].at[rows, col],
            rss[h].at[way, rs_rows(way, step), pl.ds(p * PW, PW)],
            2 + h,
            rs_sem.at[h, ag_at(way, step), p],
            z_to[way],
        )

    def rs_open(h):
        for p in range(NP):
            for way in range(2):
                rs_send(h, way, 1, p)

    def rs_wait(h, way, step, p):
        ways = way if step < 4 else pl.ds(0, 2)
        landed(rss[h].at[ways, rs_rows(way, step), pl.ds(p * PW, PW)], rs_sem.at[h, ag_at(way, step), p])

    def rs_event(h, step, p):
        dx, rs = dxs[h], rss[h]
        if step < 4:
            for way in range(2):
                rs_wait(h, way, step, p)
                shard = ring(c, (4 - step) if way == 0 else (step - 4), NZ)
                rows = pl.ds(way * HALF, HALF) if step == 1 else pl.ds(0, T)

                def body(i, carry):
                    at = lanes(shard * FB + p * (PW // BLK) + i)
                    got = rs[way, rs_rows(way, step), lanes(p * (PW // BLK) + i)]
                    dx[rows, at] = (dx[rows, at].astype(F32) + got.astype(F32)).astype(BF16)
                    return carry

                lax.fori_loop(0, PW // BLK, body, 0, unroll=2)
                rs_send(h, way, step + 1, p)
        else:
            rs_wait(h, 0, step, p)

            def body(i, carry):
                at = lanes(c * FB + p * (PW // BLK) + i)
                total = dx[:, at].astype(F32)
                for way in range(2):
                    total += rs[way, rs_rows(way, 4), lanes(p * (PW // BLK) + i)].astype(F32)
                dx[:, at] = total.astype(BF16)
                return carry

            lax.fori_loop(0, PW // BLK, body, 0, unroll=2)
            out(
                dx.at[:, pl.ds(pl.multiple_of(c * FEAT + p * PW, PW), PW)],
                gt_hbm.at[pl.ds(h * T, T), pl.ds(p * PW, PW)],
                1,
            )

    def w_at(a_, b_=0):
        return ((core * NX + a_) * NX + b_) * 6

    def pair_send(a_):
        src = dw.at[pl.ds((((1 - core) * NX + a_) * NX) * 6, 24)]
        send(src, pr.at[pl.ds(a_ * 24, 24)], 5, gc_sem.at[a_], sibling)

    def add_blocks(dst, n, *srcs):
        def body(i, carry):
            total = dw[dst + i].astype(F32)
            for ref, at in srcs:
                total += ref[at + i].astype(F32)
            dw[dst + i] = total.astype(BF16)
            return carry

        lax.fori_loop(0, n, body, 0, unroll=2)

    def pair_add(a_):
        landed(pr.at[pl.ds(a_ * 24, 24)], gc_sem.at[a_])
        add_blocks(w_at(a_), 24, (pr, a_ * 24))

    def part(buf, way, step, size):
        off = way * (size + size // 2) + (0 if step == 0 else size // 2)
        return buf.at[pl.ds(off, size // 2 if step == 0 else size)], off

    def ring_open(buf, far, size, sems, tos):
        for way in range(2):
            dst, _ = part(buf, way, 0, size)
            send(dw.at[pl.ds(far + way * (size // 2), size // 2)], dst, 5, sems.at[way, 0], tos[way])

    def ring_middle(buf, nexts, size, sems, tos):
        for way in range(2):
            got, off = part(buf, way, 0, size)
            landed(got, sems.at[way, 0])
            add_blocks(nexts[way] + way * (size // 2), size // 2, (buf, off))
            dst, _ = part(buf, way, 1, size)
            send(dw.at[pl.ds(nexts[way], size)], dst, 5, sems.at[way, 1], tos[way])

    def ring_close(buf, own, size, sems, tos):
        srcs = []
        for way in range(2):
            got, off = part(buf, way, 1, size)
            landed(got, sems.at[way, 1])
            srcs.append((buf, off))
        add_blocks(own, size, *srcs)

    a_near = (w_at(ring(a, 1, NX)), w_at(ring(a, -1, NX)))
    b_near = (w_at(a, ring(b, 1, NX)), w_at(a, ring(b, -1, NX)))

    wg[ENT] = jnp.zeros((BLK, BLK), BF16)
    tok_wait(0)
    ag_open(0)
    w_load.wait()
    w_open()
    w_near_b()
    w_near_a(0)
    w_far_b()
    ag_event(0, 1, 0)
    w_near_a(1)
    w_near_a(2)
    ag_event(0, 1, 1)
    w_near_a(3)
    w_far_a(0)
    w_far_a(1)
    w_far_a(2)
    ag_event(0, 2, 0)
    w_far_a(3)
    plan_places()
    ag_event(0, 2, 1)
    plan_table()
    ag_event(0, 3, 0)
    tok_wait(1)
    ag_event(0, 3, 1)
    ag_open(1)
    cot_load.wait()
    w_close()
    ag_event(0, 4, 0)
    ag_event(0, 4, 1)

    quarter = PAIRS // 4
    fwd(0, 0, quarter)
    ag_event(1, 1, 0)
    fwd(0, quarter, 2 * quarter)
    ag_event(1, 1, 1)
    fwd(0, 2 * quarter, 3 * quarter)
    fwd(0, 3 * quarter, PAIRS)
    ag_event(1, 2, 0)
    gelu(0)
    grad_x(0, ring(c, 4, NZ))
    ag_event(1, 2, 1)
    grad_x(0, ring(c, 3, NZ))
    grad_x(0, ring(c, -3, NZ))
    grad_x(0, ring(c, 2, NZ))
    ag_event(1, 3, 0)
    grad_x(0, ring(c, -2, NZ))
    grad_x(0, ring(c, 1, NZ))
    grad_x(0, ring(c, -1, NZ))
    grad_x(0, c)
    ag_event(1, 3, 1)
    rs_open(0)
    ag_event(1, 4, 0)
    ag_event(1, 4, 1)

    fwd(1, 0, quarter)
    rs_event(0, 1, 0)
    fwd(1, quarter, 2 * quarter)
    rs_event(0, 1, 1)
    fwd(1, 2 * quarter, 3 * quarter)
    fwd(1, 3 * quarter, PAIRS)
    gelu(1)
    rs_event(0, 2, 0)
    for g in range(2):
        grad_w(1 - core, g)
        pair_send(g)
    rs_event(0, 2, 1)
    for g in range(2, 4):
        grad_w(1 - core, g)
        pair_send(g)
    grad_w(core, ring(a, 2, NX))
    rs_event(0, 3, 0)
    grad_x(1, ring(c, 4, NZ))
    rs_open(1)
    pair_add(ring(a, 2, NX))
    ring_open(bufa, w_at(ring(a, 2, NX)), 24, ga_sem, a_to)
    grad_w(core, ring(a, 1, NX))
    grad_w(core, ring(a, -1, NX))
    rs_event(0, 3, 1)
    grad_x(1, ring(c, 3, NZ))
    grad_x(1, ring(c, -3, NZ))
    pair_add(ring(a, 1, NX))
    pair_add(ring(a, -1, NX))
    ring_middle(bufa, a_near, 24, ga_sem, a_to)
    rs_event(1, 1, 0)
    grad_w(core, a)
    pair_add(a)
    rs_event(0, 4, 0)
    grad_x(1, ring(c, 2, NZ))
    grad_x(1, ring(c, -2, NZ))
    rs_event(1, 1, 1)
    rs_event(0, 4, 1)
    grad_x(1, ring(c, 1, NZ))
    grad_x(1, ring(c, -1, NZ))
    grad_x(1, c)
    rs_event(1, 2, 0)
    ring_close(bufa, w_at(a), 24, ga_sem, a_to)
    ring_open(bufb, w_at(a, ring(b, 2, NX)), 6, gb_sem, b_to)
    rs_event(1, 2, 1)
    ring_middle(bufb, b_near, 6, gb_sem, b_to)
    rs_event(1, 3, 0)
    ring_close(bufb, w_at(a, b), 6, gb_sem, b_to)
    out(dw.at[pl.ds(w_at(a, b), 6)], gb_hbm, 2)
    rs_event(1, 3, 1)
    rs_event(1, 4, 0)
    rs_event(1, 4, 1)

    pltpu.make_async_copy(act, act_hbm, out_sem.at[0]).wait()
    pltpu.make_async_copy(dx0.at[:, pl.ds(0, CHUNKS * FEAT)], dx1.at[:, pl.ds(0, CHUNKS * FEAT)], out_sem.at[1]).wait()
    pltpu.make_async_copy(dw.at[pl.ds(0, 6)], gb_hbm, out_sem.at[2]).wait()
    for h in range(CHUNKS):
        landed(toks[h].at[pl.ds(0, 7 * FB)], send_sem.at[h])
        landed(dxs[h].at[:, pl.ds(0, 7 * FEAT)], send_sem.at[2 + h])
    landed(wg.at[pl.ds(0, 31 * 6)], send_sem.at[4])
    landed(dw.at[pl.ds(0, 31 * 6)], send_sem.at[5])


def finish(act, gt, gb, act_out, gt_out, gb_out, act_v, gt_v, gb_v, sem_in, sem_out):
    parts = [(act, act_v, act_out, pl.ds(i * 64, 64)) for i in range(4)]
    parts += [(gt, gt_v, gt_out, pl.ds(i * 128, 128)) for i in range(2)]
    parts += [(gb, gb_v, gb_out, pl.ds(0, 6))]
    loads = [pltpu.make_async_copy(src.at[at], mid.at[at], sem_in.at[i]) for i, (src, mid, _, at) in enumerate(parts)]
    stores = [pltpu.make_async_copy(mid.at[at], dst.at[at], sem_out.at[i]) for i, (_, mid, dst, at) in enumerate(parts)]
    for copy in loads:
        copy.start()
    for load, store in zip(loads, stores):
        load.wait()
        store.start()
    for copy in stores:
        copy.wait()


def on_device(tokens, weight_blocks, block_cols, cotangent):
    any_space = pl.BlockSpec(memory_space=pl.ANY)
    dma = pltpu.SemaphoreType.DMA
    act, grad_tokens, grad_blocks = pl.pallas_call(
        kernel,
        out_shape=(
            jax.ShapeDtypeStruct((CHUNKS * T, PB * BLK), BF16),
            jax.ShapeDtypeStruct((CHUNKS * T, FEAT), BF16),
            jax.ShapeDtypeStruct((6, BLK, BLK), BF16),
        ),
        in_specs=[any_space] * 4,
        out_specs=(any_space, any_space, any_space),
        scratch_shapes=[
            pltpu.VMEM((DB, T, BLK), BF16),
            pltpu.VMEM((DB, T, BLK), BF16),
            pltpu.VMEM((ENT + 1, BLK, BLK), BF16),
            pltpu.VMEM((PAIRS, T, BLK), F32),
            pltpu.VMEM((CHUNKS * T, PB * BLK), BF16),
            pltpu.VMEM((CHUNKS * T, PB * BLK), BF16),
            pltpu.VMEM((PB, T, BLK), BF16),
            pltpu.VMEM((PB, T, BLK), BF16),
            pltpu.VMEM((T, DB * BLK), BF16),
            pltpu.VMEM((T, DB * BLK), BF16),
            pltpu.VMEM((2, HALF + 3 * T, FEAT), BF16),
            pltpu.VMEM((2, HALF + 3 * T, FEAT), BF16),
            pltpu.VMEM((ENT, BLK, BLK), BF16),
            pltpu.VMEM((ENT // 2, BLK, BLK), BF16),
            pltpu.VMEM((2 * 36, BLK, BLK), BF16),
            pltpu.VMEM((2 * 9, BLK, BLK), BF16),
            pltpu.VMEM((KP, DB), jnp.int32),
            pltpu.SMEM((KP, DB), jnp.int32),
            pltpu.VMEM((8, BLK), jnp.int32),
            pltpu.SMEM((8, BLK), jnp.int32),
            pltpu.VMEM((KP, DB), jnp.int32),
            pltpu.SMEM((KP, DB), jnp.int32),
            pltpu.VMEM((32, BLK), jnp.int32),
            pltpu.SMEM((32, BLK), jnp.int32),
            dma((7,)),
            dma((3,)),
            dma((6,)),
            dma((CHUNKS, 7, NP)),
            dma((CHUNKS, 7, NP)),
            dma((3,)),
            dma((3, 4)),
            dma((1,)),
            dma((4,)),
            dma((2, 2)),
            dma((2, 2)),
        ],
        compiler_params=pltpu.CompilerParams(
            collective_id=0, has_side_effects=True, vmem_limit_bytes=60 * 1024 * 1024
        ),
        cost_estimate=pl.CostEstimate(flops=4_831_838_208, bytes_accessed=6_000_000, transcendentals=786_432),
    )(block_cols.T, tokens, weight_blocks.reshape(6, BLK, BLK), cotangent)
    act, grad_tokens, grad_blocks = pl.pallas_call(
        finish,
        out_shape=tuple(jax.ShapeDtypeStruct(v.shape, v.dtype) for v in (act, grad_tokens, grad_blocks)),
        in_specs=[any_space] * 3,
        out_specs=(any_space,) * 3,
        scratch_shapes=[*(pltpu.VMEM(v.shape, v.dtype) for v in (act, grad_tokens, grad_blocks)), dma((7,)), dma((7,))],
    )(act, grad_tokens, grad_blocks)
    return act, grad_tokens, grad_blocks.reshape(3, KP, BLK, BLK)


def solution(mesh):
    return jax.shard_map(
        on_device,
        mesh=mesh,
        in_specs=(P("row", "col"), P("row", "col", None, None), P(None, "col"), P("row", "col")),
        out_specs=(P("row", "col"), P("row", "col"), P("row", "col", None, None)),
        check_vma=False,
    )
```

```python
import jax
import jax.numpy as jnp
from jax import lax
from jax.experimental import pallas as pl
from jax.experimental.pallas import tpu as pltpu
from jax.sharding import PartitionSpec as P

MESH = pl.DeviceIdType.MESH
F32 = jnp.float32
BF16 = jnp.bfloat16

BLK = 128
PB = 24
KP = 2
DB = 96
NX = 4
NZ = 8
ENT = DB * KP
PAIRS = (ENT + PB) // 2
CHUNKS = 2
T = 128
FEAT = 1536
FB = FEAT // BLK
NP = 2
PW = FEAT // NP
HALF = T // 2

TAB_K, TAB_KEEP, TAB_LAST, TAB_W = 0, 8, 16, 24


def weight_position(k):
    r, i = k // 3, k % 3
    core = r % 2
    x = (r // 2) % NX
    y = r // (2 * NX)
    a = x + (y - x) * core
    b = y + (x - y) * core
    return (((core * NX + a) * NX + b) * 3 + i) * 2


def kernel(
    cols_hbm, tok_hbm, w_hbm, cot_hbm,
    act_hbm, gt_hbm, gb_hbm,
    tok0, tok1, wg, seg, cot, act, gp0, gp1, dx0, dx1, rs0, rs1, dw, pr, bufa, bufb,
    cols_v, cols, count_v, count, place_v, place, tab_v, tab,
    load_sem, out_sem, send_sem, ag_sem, rs_sem, wb_sem, wa_sem, wc_sem, gc_sem, ga_sem, gb_sem,
):
    toks, gps, dxs, rss = (tok0, tok1), (gp0, gp1), (dx0, dx1), (rs0, rs1)
    row, c = lax.axis_index("row"), lax.axis_index("col")
    core = row % 2
    x = (row // 2) % NX
    y = row // (2 * NX)
    a = x + (y - x) * core
    b = y + (x - y) * core

    def ring(v, step, n):
        return lax.rem(v + step + n, n)

    def chip(a_, b_):
        x_ = a_ + (b_ - a_) * core
        y_ = b_ + (a_ - b_) * core
        return ((y_ * NX + x_) * 2 + core, c)

    z_to = ((row, ring(c, 1, NZ)), (row, ring(c, -1, NZ)))
    a_to = (chip(ring(a, 1, NX), b), chip(ring(a, -1, NX), b))
    b_to = (chip(a, ring(b, 1, NX)), chip(a, ring(b, -1, NX)))
    sibling = (row + 1 - 2 * core, c)

    def remote(src, dst, sends, recv, to):
        return pltpu.make_async_remote_copy(
            src_ref=src, dst_ref=dst, send_sem=send_sem.at[sends], recv_sem=recv, device_id=to, device_id_type=MESH
        )

    def send(src, dst, sends, recv, to):
        remote(src, dst, sends, recv, to).start()

    def landed(region, recv):
        pltpu.make_async_copy(region, region, recv).wait()

    def out(src, dst, at):
        pltpu.make_async_copy(src, dst, out_sem.at[at]).start()

    w_load = pltpu.make_async_copy(w_hbm, wg.at[pl.ds(((core * NX + a) * NX + b) * 6, 6)], load_sem.at[2])
    cot_load = pltpu.make_async_copy(cot_hbm, cot, load_sem.at[3])

    def tok_load(h):
        for i in range(FB):
            pltpu.make_async_copy(
                tok_hbm.at[pl.ds(h * T, T), pl.ds(i * BLK, BLK)], toks[h].at[c * FB + i], load_sem.at[h]
            ).start()

    def tok_wait(h):
        region = toks[h].at[pl.ds(c * FB, FB)]
        pltpu.make_async_copy(region, region, load_sem.at[h]).wait()

    barrier = pltpu.get_barrier_semaphore()
    for to in (*z_to, *a_to, *b_to, sibling):
        pl.semaphore_signal(barrier, inc=1, device_id=to, device_id_type=MESH)
    tok_load(0)
    w_load.start()
    pltpu.make_async_copy(cols_hbm, cols, load_sem.at[4]).start()
    pltpu.make_async_copy(cols_hbm, cols_v, load_sem.at[5]).start()
    pl.semaphore_wait(barrier, 7)

    def ag_region(h, shard, way, step, p):
        rows = pl.ds(0, T) if step < 4 else pl.ds(way * HALF, HALF)
        return toks[h].at[pl.ds(shard * FB + p * (FB // NP), FB // NP), rows]

    def ag_at(way, step):
        return 6 if step == 4 else 2 * (step - 1) + way

    def ag_send(h, way, step, p):
        shard = ring(c, (1 - step) if way == 0 else (step - 1), NZ)
        region = ag_region(h, shard, way, step, p)
        send(region, region, h, ag_sem.at[h, ag_at(way, step), p], z_to[way])

    def ag_event(h, step, p):
        if step == 4:
            landed(ag_region(h, ring(c, 4, NZ), 0, 1, p), ag_sem.at[h, 6, p])
            return
        for way in range(2):
            shard = ring(c, -step if way == 0 else step, NZ)
            landed(ag_region(h, shard, way, step, p), ag_sem.at[h, ag_at(way, step), p])
            ag_send(h, way, step + 1, p)

    def ag_open(h):
        for p in range(NP):
            for way in range(2):
                ag_send(h, way, 1, p)

    def w_region(core_, a_, b_, lo=0, n=6):
        return wg.at[pl.ds(((core_ * NX + a_) * NX + b_) * 6 + lo, n)]

    def b_of(q):
        return ring(b, (0, 1, -1, 2)[q], NX)

    def w_to_a(q):
        region = w_region(core, a, b_of(q))
        for way in range(2):
            send(region, region, 4, wa_sem.at[way, q], a_to[way])

    def w_to_sibling(g, q):
        region = w_region(core, ring(a, (0, 1, -1, 2)[g], NX), b_of(q))
        send(region, region, 4, wc_sem.at[0], sibling)

    def w_open():
        region = w_region(core, a, b)
        for way in range(2):
            send(region, region, 4, wb_sem.at[way], b_to[way])
        w_to_a(0)
        w_to_sibling(0, 0)

    def w_near_b():
        for way in range(2):
            q = 2 if way == 0 else 1
            landed(w_region(core, a, b_of(q)), wb_sem.at[way])
            region = w_region(core, a, b_of(q), 3 * way, 3)
            send(region, region, 4, wb_sem.at[2], b_to[way])
            w_to_a(q)
            w_to_sibling(0, q)

    def w_far_b():
        landed(w_region(core, a, b_of(3)), wb_sem.at[2])
        w_to_a(3)
        w_to_sibling(0, 3)

    def w_near_a(q):
        for way in range(2):
            g = 2 if way == 0 else 1
            a_ = ring(a, -1 if way == 0 else 1, NX)
            landed(w_region(core, a_, b_of(q)), wa_sem.at[way, q])
            region = w_region(core, a_, b_of(q), 3 * way, 3)
            send(region, region, 4, wa_sem.at[2, q], a_to[way])
            w_to_sibling(g, q)

    def w_far_a(q):
        landed(w_region(core, ring(a, 2, NX), b_of(q)), wa_sem.at[2, q])
        w_to_sibling(3, q)

    def w_close():
        landed(wg.at[pl.ds((1 - core) * DB, DB)], wc_sem.at[0])

    def plan_places():
        pltpu.make_async_copy(cols_hbm, cols, load_sem.at[4]).wait()
        pltpu.make_async_copy(cols_hbm, cols_v, load_sem.at[5]).wait()
        mine = cols_v[...]
        order = lax.broadcasted_iota(jnp.int32, (KP, DB), 0) * DB + lax.broadcasted_iota(jnp.int32, (KP, DB), 1)
        lane = lax.broadcasted_iota(jnp.int32, (8, BLK), 1)

        def body(k, carry):
            at, counts = carry
            for s in range(KP):
                col = cols[s, k]
                before = (col < mine) | ((col == mine) & (s * DB + k < order))
                at = at + jnp.where(before, 1, 0)
                counts = counts + jnp.where(lane == col, 1, 0)
            return at, counts

        at, counts = lax.fori_loop(
            0, DB, body, (jnp.zeros((KP, DB), jnp.int32), jnp.zeros((8, BLK), jnp.int32)), unroll=4
        )
        count_v[...] = counts
        copy = pltpu.make_async_copy(count_v, count, load_sem.at[6])
        copy.start()
        copy.wait()
        pair = lane
        keep = jnp.ones((8, BLK), jnp.int32)
        last = jnp.full((8, BLK), -1, jnp.int32)
        base = jnp.int32(0)
        for j in range(PB):
            n = count[0, j]
            pairs = lax.shift_right_logical(n + 1, 1)
            at = at + jnp.where(mine > j, n & 1, 0)
            keep = jnp.where(pair == base, 0, keep)
            last = last + jnp.where(lane >= j, pairs, 0)
            base = base + pairs
        place_v[...] = at
        copy = pltpu.make_async_copy(place_v, place, load_sem.at[6])
        copy.start()
        copy.wait()
        tab_v[pl.ds(8, 8)] = keep
        tab_v[pl.ds(16, 8)] = last

    def plan_table():
        slot = 2 * lax.broadcasted_iota(jnp.int32, (8, BLK), 1) + lax.broadcasted_iota(jnp.int32, (8, BLK), 0)

        def body(k, carry):
            rows, where = carry
            first = weight_position(k)
            for s in range(KP):
                hit = slot == place[s, k]
                rows = jnp.where(hit, k, rows)
                where = jnp.where(hit, first + s, where)
            return rows, where

        rows, where = lax.fori_loop(
            0, DB, body, (jnp.zeros((8, BLK), jnp.int32), jnp.full((8, BLK), ENT, jnp.int32)), unroll=2
        )
        tab_v[pl.ds(0, 8)] = rows
        tab_v[pl.ds(24, 8)] = where
        copy = pltpu.make_async_copy(tab_v, tab, load_sem.at[6])
        copy.start()
        copy.wait()

    def lanes(k):
        return pl.ds(pl.multiple_of(k * BLK, BLK), BLK)

    def fwd(h, lo, hi):
        tok = toks[h]

        def body(i, acc):
            xs = jnp.concatenate([tok[tab[TAB_K + s, i]] for s in range(2)], axis=1)
            ws = jnp.concatenate([wg[tab[TAB_W + s, i]] for s in range(2)], axis=0)
            acc = acc * tab[TAB_KEEP, i].astype(F32) + jnp.dot(xs, ws, preferred_element_type=F32)
            seg[i] = acc
            return acc

        start = jnp.zeros((T, BLK), F32) if lo == 0 else seg[lo - 1]
        lax.fori_loop(lo, hi, body, start, unroll=3)

    def gelu(h):
        rows = pl.ds(h * T, T)

        def body(j, carry):
            v = seg[tab[TAB_LAST, j]]
            k0 = 0.7978845608028654
            v2 = v * v
            th = jnp.tanh(k0 * (v + 0.044715 * (v2 * v)))
            half = 0.5 * (1.0 + th)
            slope = half + (0.5 * v) * (1.0 - th * th) * (k0 * (1.0 + 3 * 0.044715 * v2))
            act[rows, lanes(j)] = (v * half).astype(BF16)
            gps[h][j] = (cot[rows, lanes(j)].astype(F32) * slope).astype(BF16)
            return carry

        lax.fori_loop(0, PB, body, 0)
        out(act.at[rows], act_hbm.at[rows], 0)

    def grad_x(h, shard):
        gp, dx = gps[h], dxs[h]

        def body(i, carry):
            k = shard * FB + i
            at = weight_position(k)
            gs = jnp.concatenate([gp[cols[s, k]] for s in range(2)], axis=1)
            ws = jnp.concatenate([wg[at + s] for s in range(2)], axis=1)
            out = lax.dot_general(gs, ws, (((1,), (1,)), ((), ())), preferred_element_type=F32)
            dx[:, lanes(k)] = out.astype(BF16)
            return carry

        lax.fori_loop(0, FB, body, 0, unroll=3)

    def grad_w(core_, a_):
        def body(i, carry):
            b_, j = i // 3, i % 3
            at = (((core_ * NX + a_) * NX + b_) * 3 + j) * 2
            x_ = a_ + (b_ - a_) * core_
            y_ = b_ + (a_ - b_) * core_
            k = ((y_ * NX + x_) * 2 + core_) * 3 + j
            xs = jnp.concatenate([tok[k] for tok in toks], axis=0)
            picks = [cols[s, k] for s in range(2)]
            gs = jnp.concatenate(
                [jnp.concatenate([gp[col] for gp in gps], axis=0) for col in picks], axis=1
            )
            out = lax.dot_general(xs, gs, (((0,), (0,)), ((), ())), preferred_element_type=F32)
            dw[at] = out[:, :BLK].astype(BF16)
            dw[at + 1] = out[:, BLK:].astype(BF16)
            return carry

        lax.fori_loop(0, 12, body, 0, unroll=2)

    def rs_rows(way, step):
        return pl.ds(0, HALF) if step == 1 else pl.ds(HALF + (step - 2) * T, T)

    def rs_send(h, way, step, p):
        shard = ring(c, (5 - step) if way == 0 else (step - 5), NZ)
        col = pl.ds(pl.multiple_of(shard * FEAT + p * PW, PW), PW)
        rows = pl.ds(way * HALF, HALF) if step == 1 else pl.ds(0, T)
        send(
            dxs[h].at[rows, col],
            rss[h].at[way, rs_rows(way, step), pl.ds(p * PW, PW)],
            2 + h,
            rs_sem.at[h, ag_at(way, step), p],
            z_to[way],
        )

    def rs_open(h):
        for p in range(NP):
            for way in range(2):
                rs_send(h, way, 1, p)

    def rs_wait(h, way, step, p):
        ways = way if step < 4 else pl.ds(0, 2)
        landed(rss[h].at[ways, rs_rows(way, step), pl.ds(p * PW, PW)], rs_sem.at[h, ag_at(way, step), p])

    def rs_event(h, step, p):
        dx, rs = dxs[h], rss[h]
        if step < 4:
            for way in range(2):
                rs_wait(h, way, step, p)
                shard = ring(c, (4 - step) if way == 0 else (step - 4), NZ)
                rows = pl.ds(way * HALF, HALF) if step == 1 else pl.ds(0, T)

                def body(i, carry):
                    at = lanes(shard * FB + p * (PW // BLK) + i)
                    got = rs[way, rs_rows(way, step), lanes(p * (PW // BLK) + i)]
                    dx[rows, at] = (dx[rows, at].astype(F32) + got.astype(F32)).astype(BF16)
                    return carry

                lax.fori_loop(0, PW // BLK, body, 0, unroll=2)
                rs_send(h, way, step + 1, p)
        else:
            rs_wait(h, 0, step, p)

            def body(i, carry):
                at = lanes(c * FB + p * (PW // BLK) + i)
                total = dx[:, at].astype(F32)
                for way in range(2):
                    total += rs[way, rs_rows(way, 4), lanes(p * (PW // BLK) + i)].astype(F32)
                dx[:, at] = total.astype(BF16)
                return carry

            lax.fori_loop(0, PW // BLK, body, 0, unroll=2)
            out(
                dx.at[:, pl.ds(pl.multiple_of(c * FEAT + p * PW, PW), PW)],
                gt_hbm.at[pl.ds(h * T, T), pl.ds(p * PW, PW)],
                1,
            )

    def w_at(a_, b_=0):
        return ((core * NX + a_) * NX + b_) * 6

    def pair_send(a_):
        src = dw.at[pl.ds((((1 - core) * NX + a_) * NX) * 6, 24)]
        send(src, pr.at[pl.ds(a_ * 24, 24)], 5, gc_sem.at[a_], sibling)

    def add_blocks(dst, n, *srcs):
        def body(i, carry):
            total = dw[dst + i].astype(F32)
            for ref, at in srcs:
                total += ref[at + i].astype(F32)
            dw[dst + i] = total.astype(BF16)
            return carry

        lax.fori_loop(0, n, body, 0, unroll=2)

    def pair_add(a_):
        landed(pr.at[pl.ds(a_ * 24, 24)], gc_sem.at[a_])
        add_blocks(w_at(a_), 24, (pr, a_ * 24))

    def part(buf, way, step, size):
        off = way * (size + size // 2) + (0 if step == 0 else size // 2)
        return buf.at[pl.ds(off, size // 2 if step == 0 else size)], off

    def ring_open(buf, far, size, sems, tos):
        for way in range(2):
            dst, _ = part(buf, way, 0, size)
            send(dw.at[pl.ds(far + way * (size // 2), size // 2)], dst, 5, sems.at[way, 0], tos[way])

    def ring_middle(buf, nexts, size, sems, tos):
        for way in range(2):
            got, off = part(buf, way, 0, size)
            landed(got, sems.at[way, 0])
            add_blocks(nexts[way] + way * (size // 2), size // 2, (buf, off))
            dst, _ = part(buf, way, 1, size)
            send(dw.at[pl.ds(nexts[way], size)], dst, 5, sems.at[way, 1], tos[way])

    def ring_close(buf, own, size, sems, tos):
        srcs = []
        for way in range(2):
            got, off = part(buf, way, 1, size)
            landed(got, sems.at[way, 1])
            srcs.append((buf, off))
        add_blocks(own, size, *srcs)

    a_near = (w_at(ring(a, 1, NX)), w_at(ring(a, -1, NX)))
    b_near = (w_at(a, ring(b, 1, NX)), w_at(a, ring(b, -1, NX)))

    wg[ENT] = jnp.zeros((BLK, BLK), BF16)
    tok_wait(0)
    ag_open(0)
    w_load.wait()
    w_open()
    tok_load(1)
    cot_load.start()
    w_near_b()
    w_near_a(0)
    ag_event(0, 1, 0)
    w_far_b()
    w_near_a(1)
    w_near_a(2)
    ag_event(0, 1, 1)
    w_near_a(3)
    w_far_a(0)
    ag_event(0, 2, 0)
    w_far_a(1)
    w_far_a(2)
    w_far_a(3)
    plan_places()
    ag_event(0, 2, 1)
    plan_table()
    ag_event(0, 3, 0)
    tok_wait(1)
    ag_event(0, 3, 1)
    ag_open(1)
    cot_load.wait()
    w_close()
    ag_event(0, 4, 0)
    ag_event(0, 4, 1)

    quarter = PAIRS // 4
    fwd(0, 0, quarter)
    ag_event(1, 1, 0)
    fwd(0, quarter, 2 * quarter)
    ag_event(1, 1, 1)
    fwd(0, 2 * quarter, 3 * quarter)
    fwd(0, 3 * quarter, PAIRS)
    ag_event(1, 2, 0)
    gelu(0)
    grad_x(0, ring(c, 4, NZ))
    ag_event(1, 2, 1)
    grad_x(0, ring(c, 3, NZ))
    grad_x(0, ring(c, -3, NZ))
    grad_x(0, ring(c, 2, NZ))
    ag_event(1, 3, 0)
    grad_x(0, ring(c, -2, NZ))
    grad_x(0, ring(c, 1, NZ))
    grad_x(0, ring(c, -1, NZ))
    grad_x(0, c)
    ag_event(1, 3, 1)
    rs_open(0)
    ag_event(1, 4, 0)
    ag_event(1, 4, 1)

    fwd(1, 0, quarter)
    rs_event(0, 1, 0)
    fwd(1, quarter, 2 * quarter)
    rs_event(0, 1, 1)
    fwd(1, 2 * quarter, 3 * quarter)
    fwd(1, 3 * quarter, PAIRS)
    gelu(1)
    rs_event(0, 2, 0)
    for g in range(2):
        grad_w(1 - core, g)
        pair_send(g)
    rs_event(0, 2, 1)
    for g in range(2, 4):
        grad_w(1 - core, g)
        pair_send(g)
    grad_w(core, ring(a, 2, NX))
    rs_event(0, 3, 0)
    grad_x(1, ring(c, 4, NZ))
    rs_open(1)
    pair_add(ring(a, 2, NX))
    ring_open(bufa, w_at(ring(a, 2, NX)), 24, ga_sem, a_to)
    grad_w(core, ring(a, 1, NX))
    grad_w(core, ring(a, -1, NX))
    rs_event(0, 3, 1)
    grad_x(1, ring(c, 3, NZ))
    grad_x(1, ring(c, -3, NZ))
    pair_add(ring(a, 1, NX))
    pair_add(ring(a, -1, NX))
    ring_middle(bufa, a_near, 24, ga_sem, a_to)
    rs_event(1, 1, 0)
    grad_w(core, a)
    pair_add(a)
    rs_event(0, 4, 0)
    grad_x(1, ring(c, 2, NZ))
    grad_x(1, ring(c, -2, NZ))
    rs_event(1, 1, 1)
    rs_event(0, 4, 1)
    grad_x(1, ring(c, 1, NZ))
    grad_x(1, ring(c, -1, NZ))
    grad_x(1, c)
    rs_event(1, 2, 0)
    ring_close(bufa, w_at(a), 24, ga_sem, a_to)
    ring_open(bufb, w_at(a, ring(b, 2, NX)), 6, gb_sem, b_to)
    rs_event(1, 2, 1)
    ring_middle(bufb, b_near, 6, gb_sem, b_to)
    rs_event(1, 3, 0)
    ring_close(bufb, w_at(a, b), 6, gb_sem, b_to)
    out(dw.at[pl.ds(w_at(a, b), 6)], gb_hbm, 2)
    rs_event(1, 3, 1)
    rs_event(1, 4, 0)
    rs_event(1, 4, 1)

    pltpu.make_async_copy(act, act_hbm, out_sem.at[0]).wait()
    pltpu.make_async_copy(dx0.at[:, pl.ds(0, CHUNKS * FEAT)], dx1.at[:, pl.ds(0, CHUNKS * FEAT)], out_sem.at[1]).wait()
    pltpu.make_async_copy(dw.at[pl.ds(0, 6)], gb_hbm, out_sem.at[2]).wait()
    for h in range(CHUNKS):
        landed(toks[h].at[pl.ds(0, 7 * FB)], send_sem.at[h])
        landed(dxs[h].at[:, pl.ds(0, 7 * FEAT)], send_sem.at[2 + h])
    landed(wg.at[pl.ds(0, 31 * 6)], send_sem.at[4])
    landed(dw.at[pl.ds(0, 31 * 6)], send_sem.at[5])


def finish(act, gt, gb, act_out, gt_out, gb_out, sem_out):
    parts = [(act, act_out, pl.ds(i * 64, 64)) for i in range(4)]
    parts += [(gt, gt_out, pl.ds(i * 128, 128)) for i in range(2)]
    parts += [(gb, gb_out, pl.ds(0, 6))]
    stores = [pltpu.make_async_copy(mid.at[at], dst.at[at], sem_out.at[i]) for i, (mid, dst, at) in enumerate(parts)]
    for copy in stores:
        copy.start()
    for copy in stores:
        copy.wait()


def on_device(tokens, weight_blocks, block_cols, cotangent):
    any_space = pl.BlockSpec(memory_space=pl.ANY)
    hbm = pl.BlockSpec(memory_space=pltpu.HBM)
    arrays = (block_cols.T, tokens, weight_blocks.reshape(6, BLK, BLK), cotangent)
    in_hbm = [pltpu.with_memory_space_constraint(v, pltpu.HBM) for v in arrays]
    dma = pltpu.SemaphoreType.DMA
    act, grad_tokens, grad_blocks = pl.pallas_call(
        kernel,
        out_shape=(
            jax.ShapeDtypeStruct((CHUNKS * T, PB * BLK), BF16),
            jax.ShapeDtypeStruct((CHUNKS * T, FEAT), BF16),
            jax.ShapeDtypeStruct((6, BLK, BLK), BF16),
        ),
        in_specs=[hbm] * 4,
        out_specs=(any_space, any_space, any_space),
        scratch_shapes=[
            pltpu.VMEM((DB, T, BLK), BF16),
            pltpu.VMEM((DB, T, BLK), BF16),
            pltpu.VMEM((ENT + 1, BLK, BLK), BF16),
            pltpu.VMEM((PAIRS, T, BLK), F32),
            pltpu.VMEM((CHUNKS * T, PB * BLK), BF16),
            pltpu.VMEM((CHUNKS * T, PB * BLK), BF16),
            pltpu.VMEM((PB, T, BLK), BF16),
            pltpu.VMEM((PB, T, BLK), BF16),
            pltpu.VMEM((T, DB * BLK), BF16),
            pltpu.VMEM((T, DB * BLK), BF16),
            pltpu.VMEM((2, HALF + 3 * T, FEAT), BF16),
            pltpu.VMEM((2, HALF + 3 * T, FEAT), BF16),
            pltpu.VMEM((ENT, BLK, BLK), BF16),
            pltpu.VMEM((ENT // 2, BLK, BLK), BF16),
            pltpu.VMEM((2 * 36, BLK, BLK), BF16),
            pltpu.VMEM((2 * 9, BLK, BLK), BF16),
            pltpu.VMEM((KP, DB), jnp.int32),
            pltpu.SMEM((KP, DB), jnp.int32),
            pltpu.VMEM((8, BLK), jnp.int32),
            pltpu.SMEM((8, BLK), jnp.int32),
            pltpu.VMEM((KP, DB), jnp.int32),
            pltpu.SMEM((KP, DB), jnp.int32),
            pltpu.VMEM((32, BLK), jnp.int32),
            pltpu.SMEM((32, BLK), jnp.int32),
            dma((7,)),
            dma((3,)),
            dma((6,)),
            dma((CHUNKS, 7, NP)),
            dma((CHUNKS, 7, NP)),
            dma((3,)),
            dma((3, 4)),
            dma((1,)),
            dma((4,)),
            dma((2, 2)),
            dma((2, 2)),
        ],
        compiler_params=pltpu.CompilerParams(
            collective_id=0, has_side_effects=True, vmem_limit_bytes=50 * 1024 * 1024
        ),
        cost_estimate=pl.CostEstimate(flops=4_831_838_208, bytes_accessed=6_000_000, transcendentals=786_432),
    )(*in_hbm)
    act, grad_tokens, grad_blocks = pl.pallas_call(
        finish,
        out_shape=tuple(jax.ShapeDtypeStruct(v.shape, v.dtype) for v in (act, grad_tokens, grad_blocks)),
        in_specs=[any_space] * 3,
        out_specs=(hbm,) * 3,
        scratch_shapes=[dma((7,))],
        compiler_params=pltpu.CompilerParams(vmem_limit_bytes=1024 * 1024),
    )(act, grad_tokens, grad_blocks)
    return act, grad_tokens, grad_blocks.reshape(3, KP, BLK, BLK)


def solution(mesh):
    return jax.shard_map(
        on_device,
        mesh=mesh,
        in_specs=(P("row", "col"), P("row", "col", None, None), P(None, "col"), P("row", "col")),
        out_specs=(P("row", "col"), P("row", "col"), P("row", "col", None, None)),
        check_vma=False,
    )
```

```python
import jax
import jax.numpy as jnp
from jax import lax
from jax.experimental import pallas as pl
from jax.experimental.pallas import tpu as pltpu
from jax.sharding import PartitionSpec as P

MESH = pl.DeviceIdType.MESH
F32 = jnp.float32
BF16 = jnp.bfloat16

BLK = 128
PB = 24
KP = 2
DB = 96
NX = 4
NZ = 8
ENT = DB * KP
PAIRS = (ENT + PB) // 2
CHUNKS = 2
T = 128
FEAT = 1536
FB = FEAT // BLK
NP = 2
PW = FEAT // NP
HALF = T // 2

TAB_K, TAB_KEEP, TAB_LAST, TAB_W = 0, 8, 16, 24


def weight_position(k):
    r, i = k // 3, k % 3
    core = r % 2
    x = (r // 2) % NX
    y = r // (2 * NX)
    a = x + (y - x) * core
    b = y + (x - y) * core
    return (((core * NX + a) * NX + b) * 3 + i) * 2


def kernel(
    cols_hbm, tok_hbm, w_hbm, cot_hbm,
    act_hbm, gt_hbm, gb_hbm,
    tok0, tok1, wg, seg, cot, act, gp0, gp1, dx0, dx1, rs0, rs1, dw, pr, bufa, bufb,
    cols_v, cols, count_v, count, place_v, place, tab_v, tab,
    load_sem, out_sem, send_sem, ag_sem, rs_sem, wb_sem, wa_sem, wc_sem, gc_sem, ga_sem, gb_sem,
):
    toks, gps, dxs, rss = (tok0, tok1), (gp0, gp1), (dx0, dx1), (rs0, rs1)
    row, c = lax.axis_index("row"), lax.axis_index("col")
    core = row % 2
    x = (row // 2) % NX
    y = row // (2 * NX)
    a = x + (y - x) * core
    b = y + (x - y) * core

    def ring(v, step, n):
        return lax.rem(v + step + n, n)

    def chip(a_, b_):
        x_ = a_ + (b_ - a_) * core
        y_ = b_ + (a_ - b_) * core
        return ((y_ * NX + x_) * 2 + core, c)

    z_to = ((row, ring(c, 1, NZ)), (row, ring(c, -1, NZ)))
    a_to = (chip(ring(a, 1, NX), b), chip(ring(a, -1, NX), b))
    b_to = (chip(a, ring(b, 1, NX)), chip(a, ring(b, -1, NX)))
    sibling = (row + 1 - 2 * core, c)

    def remote(src, dst, sends, recv, to):
        return pltpu.make_async_remote_copy(
            src_ref=src, dst_ref=dst, send_sem=send_sem.at[sends], recv_sem=recv, device_id=to, device_id_type=MESH
        )

    def send(src, dst, sends, recv, to):
        remote(src, dst, sends, recv, to).start()

    def landed(region, recv):
        pltpu.make_async_copy(region, region, recv).wait()

    def out(src, dst, at):
        pltpu.make_async_copy(src, dst, out_sem.at[at]).start()

    w_load = pltpu.make_async_copy(w_hbm, wg.at[pl.ds(((core * NX + a) * NX + b) * 6, 6)], load_sem.at[2])
    cot_load = pltpu.make_async_copy(cot_hbm, cot, load_sem.at[3])

    def tok_load(h):
        for i in range(FB):
            pltpu.make_async_copy(
                tok_hbm.at[pl.ds(h * T, T), pl.ds(i * BLK, BLK)], toks[h].at[c * FB + i], load_sem.at[h]
            ).start()

    def tok_wait(h):
        region = toks[h].at[pl.ds(c * FB, FB)]
        pltpu.make_async_copy(region, region, load_sem.at[h]).wait()

    barrier = pltpu.get_barrier_semaphore()
    for to in (*z_to, *a_to, *b_to, sibling):
        pl.semaphore_signal(barrier, inc=1, device_id=to, device_id_type=MESH)
    tok_load(0)
    w_load.start()
    pltpu.make_async_copy(cols_hbm, cols, load_sem.at[4]).start()
    pltpu.make_async_copy(cols_hbm, cols_v, load_sem.at[5]).start()
    pl.semaphore_wait(barrier, 7)

    def ag_region(h, shard, way, step, p):
        rows = pl.ds(0, T) if step < 4 else pl.ds(way * HALF, HALF)
        return toks[h].at[pl.ds(shard * FB + p * (FB // NP), FB // NP), rows]

    def ag_at(way, step):
        return 6 if step == 4 else 2 * (step - 1) + way

    def ag_send(h, way, step, p):
        shard = ring(c, (1 - step) if way == 0 else (step - 1), NZ)
        region = ag_region(h, shard, way, step, p)
        send(region, region, h, ag_sem.at[h, ag_at(way, step), p], z_to[way])

    def ag_event(h, step, p):
        if step == 4:
            landed(ag_region(h, ring(c, 4, NZ), 0, 1, p), ag_sem.at[h, 6, p])
            return
        for way in range(2):
            shard = ring(c, -step if way == 0 else step, NZ)
            landed(ag_region(h, shard, way, step, p), ag_sem.at[h, ag_at(way, step), p])
            ag_send(h, way, step + 1, p)

    def ag_open(h):
        for p in range(NP):
            for way in range(2):
                ag_send(h, way, 1, p)

    def w_region(core_, a_, b_, lo=0, n=6):
        return wg.at[pl.ds(((core_ * NX + a_) * NX + b_) * 6 + lo, n)]

    def b_of(q):
        return ring(b, (0, 1, -1, 2)[q], NX)

    def w_to_a(q):
        region = w_region(core, a, b_of(q))
        for way in range(2):
            send(region, region, 4, wa_sem.at[way, q], a_to[way])

    def w_to_sibling(g, q):
        region = w_region(core, ring(a, (0, 1, -1, 2)[g], NX), b_of(q))
        send(region, region, 4, wc_sem.at[0], sibling)

    def w_open():
        region = w_region(core, a, b)
        for way in range(2):
            send(region, region, 4, wb_sem.at[way], b_to[way])
        w_to_a(0)
        w_to_sibling(0, 0)

    def w_near_b():
        for way in range(2):
            q = 2 if way == 0 else 1
            landed(w_region(core, a, b_of(q)), wb_sem.at[way])
            region = w_region(core, a, b_of(q), 3 * way, 3)
            send(region, region, 4, wb_sem.at[2], b_to[way])
            w_to_a(q)
            w_to_sibling(0, q)

    def w_far_b():
        landed(w_region(core, a, b_of(3)), wb_sem.at[2])
        w_to_a(3)
        w_to_sibling(0, 3)

    def w_near_a(q):
        for way in range(2):
            g = 2 if way == 0 else 1
            a_ = ring(a, -1 if way == 0 else 1, NX)
            landed(w_region(core, a_, b_of(q)), wa_sem.at[way, q])
            region = w_region(core, a_, b_of(q), 3 * way, 3)
            send(region, region, 4, wa_sem.at[2, q], a_to[way])
            w_to_sibling(g, q)

    def w_far_a(q):
        landed(w_region(core, ring(a, 2, NX), b_of(q)), wa_sem.at[2, q])
        w_to_sibling(3, q)

    def w_close():
        landed(wg.at[pl.ds((1 - core) * DB, DB)], wc_sem.at[0])

    def plan_places():
        pltpu.make_async_copy(cols_hbm, cols, load_sem.at[4]).wait()
        pltpu.make_async_copy(cols_hbm, cols_v, load_sem.at[5]).wait()
        mine = cols_v[...]
        order = lax.broadcasted_iota(jnp.int32, (KP, DB), 0) * DB + lax.broadcasted_iota(jnp.int32, (KP, DB), 1)
        lane = lax.broadcasted_iota(jnp.int32, (8, BLK), 1)

        def body(k, carry):
            at, counts = carry
            for s in range(KP):
                col = cols[s, k]
                before = (col < mine) | ((col == mine) & (s * DB + k < order))
                at = at + jnp.where(before, 1, 0)
                counts = counts + jnp.where(lane == col, 1, 0)
            return at, counts

        at, counts = lax.fori_loop(
            0, DB, body, (jnp.zeros((KP, DB), jnp.int32), jnp.zeros((8, BLK), jnp.int32)), unroll=4
        )
        count_v[...] = counts
        copy = pltpu.make_async_copy(count_v, count, load_sem.at[6])
        copy.start()
        copy.wait()
        pair = lane
        keep = jnp.ones((8, BLK), jnp.int32)
        last = jnp.full((8, BLK), -1, jnp.int32)
        base = jnp.int32(0)
        for j in range(PB):
            n = count[0, j]
            pairs = lax.shift_right_logical(n + 1, 1)
            at = at + jnp.where(mine > j, n & 1, 0)
            keep = jnp.where(pair == base, 0, keep)
            last = last + jnp.where(lane >= j, pairs, 0)
            base = base + pairs
        place_v[...] = at
        copy = pltpu.make_async_copy(place_v, place, load_sem.at[6])
        copy.start()
        copy.wait()
        tab_v[pl.ds(8, 8)] = keep
        tab_v[pl.ds(16, 8)] = last

    def plan_table():
        slot = 2 * lax.broadcasted_iota(jnp.int32, (8, BLK), 1) + lax.broadcasted_iota(jnp.int32, (8, BLK), 0)

        def body(k, carry):
            rows, where = carry
            first = weight_position(k)
            for s in range(KP):
                hit = slot == place[s, k]
                rows = jnp.where(hit, k, rows)
                where = jnp.where(hit, first + s, where)
            return rows, where

        rows, where = lax.fori_loop(
            0, DB, body, (jnp.zeros((8, BLK), jnp.int32), jnp.full((8, BLK), ENT, jnp.int32)), unroll=2
        )
        tab_v[pl.ds(0, 8)] = rows
        tab_v[pl.ds(24, 8)] = where
        copy = pltpu.make_async_copy(tab_v, tab, load_sem.at[6])
        copy.start()
        copy.wait()

    def lanes(k):
        return pl.ds(pl.multiple_of(k * BLK, BLK), BLK)

    def fwd(h, lo, hi):
        tok = toks[h]

        def body(i, acc):
            xs = jnp.concatenate([tok[tab[TAB_K + s, i]] for s in range(2)], axis=1)
            ws = jnp.concatenate([wg[tab[TAB_W + s, i]] for s in range(2)], axis=0)
            acc = acc * tab[TAB_KEEP, i].astype(F32) + jnp.dot(xs, ws, preferred_element_type=F32)
            seg[i] = acc
            return acc

        start = jnp.zeros((T, BLK), F32) if lo == 0 else seg[lo - 1]
        lax.fori_loop(lo, hi, body, start, unroll=3)

    def gelu(h):
        rows = pl.ds(h * T, T)

        def body(j, carry):
            v = seg[tab[TAB_LAST, j]]
            k0 = 0.7978845608028654
            v2 = v * v
            th = jnp.tanh(k0 * (v + 0.044715 * (v2 * v)))
            half = 0.5 * (1.0 + th)
            slope = half + (0.5 * v) * (1.0 - th * th) * (k0 * (1.0 + 3 * 0.044715 * v2))
            act[rows, lanes(j)] = (v * half).astype(BF16)
            gps[h][j] = (cot[rows, lanes(j)].astype(F32) * slope).astype(BF16)
            return carry

        lax.fori_loop(0, PB, body, 0)
        out(act.at[rows], act_hbm.at[rows], 0)

    def grad_x(h, shard):
        gp, dx = gps[h], dxs[h]

        def body(i, carry):
            k = shard * FB + i
            at = weight_position(k)
            gs = jnp.concatenate([gp[cols[s, k]] for s in range(2)], axis=1)
            ws = jnp.concatenate([wg[at + s] for s in range(2)], axis=1)
            out = lax.dot_general(gs, ws, (((1,), (1,)), ((), ())), preferred_element_type=F32)
            dx[:, lanes(k)] = out.astype(BF16)
            return carry

        lax.fori_loop(0, FB, body, 0, unroll=3)

    def grad_w(core_, a_):
        def body(i, carry):
            b_, j = i // 3, i % 3
            at = (((core_ * NX + a_) * NX + b_) * 3 + j) * 2
            x_ = a_ + (b_ - a_) * core_
            y_ = b_ + (a_ - b_) * core_
            k = ((y_ * NX + x_) * 2 + core_) * 3 + j
            xs = jnp.concatenate([tok[k] for tok in toks], axis=0)
            picks = [cols[s, k] for s in range(2)]
            gs = jnp.concatenate(
                [jnp.concatenate([gp[col] for gp in gps], axis=0) for col in picks], axis=1
            )
            out = lax.dot_general(xs, gs, (((0,), (0,)), ((), ())), preferred_element_type=F32)
            dw[at] = out[:, :BLK].astype(BF16)
            dw[at + 1] = out[:, BLK:].astype(BF16)
            return carry

        lax.fori_loop(0, 12, body, 0, unroll=2)

    def rs_rows(way, step):
        return pl.ds(0, HALF) if step == 1 else pl.ds(HALF + (step - 2) * T, T)

    def rs_send(h, way, step, p):
        shard = ring(c, (5 - step) if way == 0 else (step - 5), NZ)
        col = pl.ds(pl.multiple_of(shard * FEAT + p * PW, PW), PW)
        rows = pl.ds(way * HALF, HALF) if step == 1 else pl.ds(0, T)
        send(
            dxs[h].at[rows, col],
            rss[h].at[way, rs_rows(way, step), pl.ds(p * PW, PW)],
            2 + h,
            rs_sem.at[h, ag_at(way, step), p],
            z_to[way],
        )

    def rs_open(h):
        for p in range(NP):
            for way in range(2):
                rs_send(h, way, 1, p)

    def rs_wait(h, way, step, p):
        ways = way if step < 4 else pl.ds(0, 2)
        landed(rss[h].at[ways, rs_rows(way, step), pl.ds(p * PW, PW)], rs_sem.at[h, ag_at(way, step), p])

    def rs_event(h, step, p):
        dx, rs = dxs[h], rss[h]
        if step < 4:
            for way in range(2):
                rs_wait(h, way, step, p)
                shard = ring(c, (4 - step) if way == 0 else (step - 4), NZ)
                rows = pl.ds(way * HALF, HALF) if step == 1 else pl.ds(0, T)

                def body(i, carry):
                    at = lanes(shard * FB + p * (PW // BLK) + i)
                    got = rs[way, rs_rows(way, step), lanes(p * (PW // BLK) + i)]
                    dx[rows, at] = (dx[rows, at].astype(F32) + got.astype(F32)).astype(BF16)
                    return carry

                lax.fori_loop(0, PW // BLK, body, 0, unroll=2)
                rs_send(h, way, step + 1, p)
        else:
            rs_wait(h, 0, step, p)

            def body(i, carry):
                at = lanes(c * FB + p * (PW // BLK) + i)
                total = dx[:, at].astype(F32)
                for way in range(2):
                    total += rs[way, rs_rows(way, 4), lanes(p * (PW // BLK) + i)].astype(F32)
                dx[:, at] = total.astype(BF16)
                return carry

            lax.fori_loop(0, PW // BLK, body, 0, unroll=2)
            out(
                dx.at[:, pl.ds(pl.multiple_of(c * FEAT + p * PW, PW), PW)],
                gt_hbm.at[pl.ds(h * T, T), pl.ds(p * PW, PW)],
                1,
            )

    def w_at(a_, b_=0):
        return ((core * NX + a_) * NX + b_) * 6

    def pair_send(a_):
        src = dw.at[pl.ds((((1 - core) * NX + a_) * NX) * 6, 24)]
        send(src, pr.at[pl.ds(a_ * 24, 24)], 5, gc_sem.at[a_], sibling)

    def add_blocks(dst, n, *srcs):
        def body(i, carry):
            total = dw[dst + i].astype(F32)
            for ref, at in srcs:
                total += ref[at + i].astype(F32)
            dw[dst + i] = total.astype(BF16)
            return carry

        lax.fori_loop(0, n, body, 0, unroll=2)

    def pair_add(a_):
        landed(pr.at[pl.ds(a_ * 24, 24)], gc_sem.at[a_])
        add_blocks(w_at(a_), 24, (pr, a_ * 24))

    def part(buf, way, step, size):
        off = way * (size + size // 2) + (0 if step == 0 else size // 2)
        return buf.at[pl.ds(off, size // 2 if step == 0 else size)], off

    def ring_open(buf, far, size, sems, tos):
        for way in range(2):
            dst, _ = part(buf, way, 0, size)
            send(dw.at[pl.ds(far + way * (size // 2), size // 2)], dst, 5, sems.at[way, 0], tos[way])

    def ring_middle(buf, nexts, size, sems, tos):
        for way in range(2):
            got, off = part(buf, way, 0, size)
            landed(got, sems.at[way, 0])
            add_blocks(nexts[way] + way * (size // 2), size // 2, (buf, off))
            dst, _ = part(buf, way, 1, size)
            send(dw.at[pl.ds(nexts[way], size)], dst, 5, sems.at[way, 1], tos[way])

    def ring_close(buf, own, size, sems, tos):
        srcs = []
        for way in range(2):
            got, off = part(buf, way, 1, size)
            landed(got, sems.at[way, 1])
            srcs.append((buf, off))
        add_blocks(own, size, *srcs)

    a_near = (w_at(ring(a, 1, NX)), w_at(ring(a, -1, NX)))
    b_near = (w_at(a, ring(b, 1, NX)), w_at(a, ring(b, -1, NX)))

    wg[ENT] = jnp.zeros((BLK, BLK), BF16)
    tok_wait(0)
    ag_open(0)
    w_load.wait()
    w_open()
    tok_load(1)
    cot_load.start()
    ag_event(0, 1, 0)
    w_near_b()
    w_near_a(0)
    ag_event(0, 1, 1)
    w_far_b()
    ag_event(0, 2, 0)
    w_near_a(1)
    w_near_a(2)
    ag_event(0, 2, 1)
    w_near_a(3)
    w_far_a(0)
    ag_event(0, 3, 0)
    w_far_a(1)
    w_far_a(2)
    w_far_a(3)
    tok_wait(1)
    ag_event(0, 3, 1)
    ag_open(1)
    plan_places()
    plan_table()
    cot_load.wait()
    w_close()
    ag_event(0, 4, 0)
    ag_event(0, 4, 1)

    quarter = PAIRS // 4
    fwd(0, 0, quarter)
    ag_event(1, 1, 0)
    fwd(0, quarter, 2 * quarter)
    ag_event(1, 1, 1)
    fwd(0, 2 * quarter, 3 * quarter)
    fwd(0, 3 * quarter, PAIRS)
    ag_event(1, 2, 0)
    gelu(0)
    grad_x(0, ring(c, 4, NZ))
    ag_event(1, 2, 1)
    grad_x(0, ring(c, 3, NZ))
    grad_x(0, ring(c, -3, NZ))
    grad_x(0, ring(c, 2, NZ))
    ag_event(1, 3, 0)
    grad_x(0, ring(c, -2, NZ))
    grad_x(0, ring(c, 1, NZ))
    grad_x(0, ring(c, -1, NZ))
    grad_x(0, c)
    ag_event(1, 3, 1)
    rs_open(0)
    ag_event(1, 4, 0)
    ag_event(1, 4, 1)

    fwd(1, 0, quarter)
    rs_event(0, 1, 0)
    fwd(1, quarter, 2 * quarter)
    rs_event(0, 1, 1)
    fwd(1, 2 * quarter, 3 * quarter)
    fwd(1, 3 * quarter, PAIRS)
    gelu(1)
    rs_event(0, 2, 0)
    for g in range(2):
        grad_w(1 - core, g)
        pair_send(g)
    rs_event(0, 2, 1)
    for g in range(2, 4):
        grad_w(1 - core, g)
        pair_send(g)
    grad_w(core, ring(a, 2, NX))
    rs_event(0, 3, 0)
    grad_x(1, ring(c, 4, NZ))
    rs_open(1)
    pair_add(ring(a, 2, NX))
    ring_open(bufa, w_at(ring(a, 2, NX)), 24, ga_sem, a_to)
    grad_w(core, ring(a, 1, NX))
    grad_w(core, ring(a, -1, NX))
    rs_event(0, 3, 1)
    grad_x(1, ring(c, 3, NZ))
    grad_x(1, ring(c, -3, NZ))
    pair_add(ring(a, 1, NX))
    pair_add(ring(a, -1, NX))
    ring_middle(bufa, a_near, 24, ga_sem, a_to)
    rs_event(1, 1, 0)
    grad_w(core, a)
    pair_add(a)
    rs_event(0, 4, 0)
    grad_x(1, ring(c, 2, NZ))
    grad_x(1, ring(c, -2, NZ))
    rs_event(1, 1, 1)
    rs_event(0, 4, 1)
    grad_x(1, ring(c, 1, NZ))
    grad_x(1, ring(c, -1, NZ))
    grad_x(1, c)
    rs_event(1, 2, 0)
    ring_close(bufa, w_at(a), 24, ga_sem, a_to)
    ring_open(bufb, w_at(a, ring(b, 2, NX)), 6, gb_sem, b_to)
    rs_event(1, 2, 1)
    ring_middle(bufb, b_near, 6, gb_sem, b_to)
    rs_event(1, 3, 0)
    ring_close(bufb, w_at(a, b), 6, gb_sem, b_to)
    out(dw.at[pl.ds(w_at(a, b), 6)], gb_hbm, 2)
    rs_event(1, 3, 1)
    rs_event(1, 4, 0)
    rs_event(1, 4, 1)

    pltpu.make_async_copy(act, act_hbm, out_sem.at[0]).wait()
    pltpu.make_async_copy(dx0.at[:, pl.ds(0, CHUNKS * FEAT)], dx1.at[:, pl.ds(0, CHUNKS * FEAT)], out_sem.at[1]).wait()
    pltpu.make_async_copy(dw.at[pl.ds(0, 6)], gb_hbm, out_sem.at[2]).wait()
    for h in range(CHUNKS):
        landed(toks[h].at[pl.ds(0, 7 * FB)], send_sem.at[h])
        landed(dxs[h].at[:, pl.ds(0, 7 * FEAT)], send_sem.at[2 + h])
    landed(wg.at[pl.ds(0, 31 * 6)], send_sem.at[4])
    landed(dw.at[pl.ds(0, 31 * 6)], send_sem.at[5])


def finish(act, gt, gb, act_out, gt_out, gb_out, sem_out):
    parts = [(act, act_out, pl.ds(i * 64, 64)) for i in range(4)]
    parts += [(gt, gt_out, pl.ds(i * 128, 128)) for i in range(2)]
    parts += [(gb, gb_out, pl.ds(0, 6))]
    stores = [pltpu.make_async_copy(mid.at[at], dst.at[at], sem_out.at[i]) for i, (mid, dst, at) in enumerate(parts)]
    for copy in stores:
        copy.start()
    for copy in stores:
        copy.wait()


def on_device(tokens, weight_blocks, block_cols, cotangent):
    any_space = pl.BlockSpec(memory_space=pl.ANY)
    hbm = pl.BlockSpec(memory_space=pltpu.HBM)
    arrays = (block_cols.T, tokens, weight_blocks.reshape(6, BLK, BLK), cotangent)
    in_hbm = [pltpu.with_memory_space_constraint(v, pltpu.HBM) for v in arrays]
    dma = pltpu.SemaphoreType.DMA
    act, grad_tokens, grad_blocks = pl.pallas_call(
        kernel,
        out_shape=(
            jax.ShapeDtypeStruct((CHUNKS * T, PB * BLK), BF16),
            jax.ShapeDtypeStruct((CHUNKS * T, FEAT), BF16),
            jax.ShapeDtypeStruct((6, BLK, BLK), BF16),
        ),
        in_specs=[hbm] * 4,
        out_specs=(any_space, any_space, any_space),
        scratch_shapes=[
            pltpu.VMEM((DB, T, BLK), BF16),
            pltpu.VMEM((DB, T, BLK), BF16),
            pltpu.VMEM((ENT + 1, BLK, BLK), BF16),
            pltpu.VMEM((PAIRS, T, BLK), F32),
            pltpu.VMEM((CHUNKS * T, PB * BLK), BF16),
            pltpu.VMEM((CHUNKS * T, PB * BLK), BF16),
            pltpu.VMEM((PB, T, BLK), BF16),
            pltpu.VMEM((PB, T, BLK), BF16),
            pltpu.VMEM((T, DB * BLK), BF16),
            pltpu.VMEM((T, DB * BLK), BF16),
            pltpu.VMEM((2, HALF + 3 * T, FEAT), BF16),
            pltpu.VMEM((2, HALF + 3 * T, FEAT), BF16),
            pltpu.VMEM((ENT, BLK, BLK), BF16),
            pltpu.VMEM((ENT // 2, BLK, BLK), BF16),
            pltpu.VMEM((2 * 36, BLK, BLK), BF16),
            pltpu.VMEM((2 * 9, BLK, BLK), BF16),
            pltpu.VMEM((KP, DB), jnp.int32),
            pltpu.SMEM((KP, DB), jnp.int32),
            pltpu.VMEM((8, BLK), jnp.int32),
            pltpu.SMEM((8, BLK), jnp.int32),
            pltpu.VMEM((KP, DB), jnp.int32),
            pltpu.SMEM((KP, DB), jnp.int32),
            pltpu.VMEM((32, BLK), jnp.int32),
            pltpu.SMEM((32, BLK), jnp.int32),
            dma((7,)),
            dma((3,)),
            dma((6,)),
            dma((CHUNKS, 7, NP)),
            dma((CHUNKS, 7, NP)),
            dma((3,)),
            dma((3, 4)),
            dma((1,)),
            dma((4,)),
            dma((2, 2)),
            dma((2, 2)),
        ],
        compiler_params=pltpu.CompilerParams(
            collective_id=0, has_side_effects=True, vmem_limit_bytes=50 * 1024 * 1024
        ),
        cost_estimate=pl.CostEstimate(flops=4_831_838_208, bytes_accessed=6_000_000, transcendentals=786_432),
    )(*in_hbm)
    act, grad_tokens, grad_blocks = pl.pallas_call(
        finish,
        out_shape=tuple(jax.ShapeDtypeStruct(v.shape, v.dtype) for v in (act, grad_tokens, grad_blocks)),
        in_specs=[any_space] * 3,
        out_specs=(hbm,) * 3,
        scratch_shapes=[dma((7,))],
        compiler_params=pltpu.CompilerParams(vmem_limit_bytes=1024 * 1024),
    )(act, grad_tokens, grad_blocks)
    return act, grad_tokens, grad_blocks.reshape(3, KP, BLK, BLK)


def solution(mesh):
    return jax.shard_map(
        on_device,
        mesh=mesh,
        in_specs=(P("row", "col"), P("row", "col", None, None), P(None, "col"), P("row", "col")),
        out_specs=(P("row", "col"), P("row", "col"), P("row", "col", None, None)),
        check_vma=False,
    )
```

```python
import jax
import jax.numpy as jnp
from jax import lax
from jax.experimental import pallas as pl
from jax.experimental.pallas import tpu as pltpu
from jax.sharding import PartitionSpec as P

MESH = pl.DeviceIdType.MESH
F32 = jnp.float32
BF16 = jnp.bfloat16

BLK = 128
PB = 24
KP = 2
DB = 96
NX = 4
NZ = 8
ENT = DB * KP
PAIRS = (ENT + PB) // 2
CHUNKS = 2
T = 128
FEAT = 1536
FB = FEAT // BLK
NP = 2
PW = FEAT // NP
HALF = T // 2

TAB_K, TAB_KEEP, TAB_LAST, TAB_W = 0, 8, 16, 24


def weight_position(k):
    r, i = k // 3, k % 3
    core = r % 2
    x = (r // 2) % NX
    y = r // (2 * NX)
    a = x + (y - x) * core
    b = y + (x - y) * core
    return (((core * NX + a) * NX + b) * 3 + i) * 2


def kernel(
    cols_hbm, tok_hbm, w_hbm, cot_hbm,
    act_hbm, gt_hbm, gb_hbm,
    tok0, tok1, wg, seg, cot, act, gp0, gp1, dx0, dx1, rs0, rs1, dw, pr, bufa, bufb,
    cols_v, cols, count_v, count, place_v, place, tab_v, tab,
    load_sem, out_sem, send_sem, ag_sem, rs_sem, wb_sem, wa_sem, wc_sem, gc_sem, ga_sem, gb_sem,
):
    toks, gps, dxs, rss = (tok0, tok1), (gp0, gp1), (dx0, dx1), (rs0, rs1)
    row, c = lax.axis_index("row"), lax.axis_index("col")
    core = row % 2
    x = (row // 2) % NX
    y = row // (2 * NX)
    a = x + (y - x) * core
    b = y + (x - y) * core

    def ring(v, step, n):
        return lax.rem(v + step + n, n)

    def chip(a_, b_):
        x_ = a_ + (b_ - a_) * core
        y_ = b_ + (a_ - b_) * core
        return ((y_ * NX + x_) * 2 + core, c)

    z_to = ((row, ring(c, 1, NZ)), (row, ring(c, -1, NZ)))
    a_to = (chip(ring(a, 1, NX), b), chip(ring(a, -1, NX), b))
    b_to = (chip(a, ring(b, 1, NX)), chip(a, ring(b, -1, NX)))
    sibling = (row + 1 - 2 * core, c)

    def remote(src, dst, sends, recv, to):
        return pltpu.make_async_remote_copy(
            src_ref=src, dst_ref=dst, send_sem=send_sem.at[sends], recv_sem=recv, device_id=to, device_id_type=MESH
        )

    def send(src, dst, sends, recv, to):
        remote(src, dst, sends, recv, to).start()

    def landed(region, recv):
        pltpu.make_async_copy(region, region, recv).wait()

    def out(src, dst, at):
        pltpu.make_async_copy(src, dst, out_sem.at[at]).start()

    w_load = pltpu.make_async_copy(w_hbm, wg.at[pl.ds(((core * NX + a) * NX + b) * 6, 6)], load_sem.at[2])
    cot_load = pltpu.make_async_copy(cot_hbm, cot, load_sem.at[3])

    def tok_load(h):
        for i in range(FB):
            pltpu.make_async_copy(
                tok_hbm.at[pl.ds(h * T, T), pl.ds(i * BLK, BLK)], toks[h].at[c * FB + i], load_sem.at[h]
            ).start()

    def tok_wait(h):
        region = toks[h].at[pl.ds(c * FB, FB)]
        pltpu.make_async_copy(region, region, load_sem.at[h]).wait()

    barrier = pltpu.get_barrier_semaphore()
    for to in (*z_to, *a_to, *b_to, sibling):
        pl.semaphore_signal(barrier, inc=1, device_id=to, device_id_type=MESH)
    tok_load(0)
    w_load.start()
    pltpu.make_async_copy(cols_hbm, cols, load_sem.at[4]).start()
    pltpu.make_async_copy(cols_hbm, cols_v, load_sem.at[5]).start()
    pl.semaphore_wait(barrier, 7)

    def ag_region(h, shard, way, step, p):
        rows = pl.ds(0, T) if step < 4 else pl.ds(way * HALF, HALF)
        return toks[h].at[pl.ds(shard * FB + p * (FB // NP), FB // NP), rows]

    def ag_send(h, way, step, p):
        shard = ring(c, (1 - step) if way == 0 else (step - 1), NZ)
        region = ag_region(h, shard, way, step, p)
        send(region, region, h, ag_sem.at[h, step - 1, p], z_to[way])

    def ag_event(h, step, p):
        n = FB // NP if step == 4 else 2 * FB // NP
        landed(toks[h].at[pl.ds(0, n)], ag_sem.at[h, step - 1, p])
        if step < 4:
            for way in range(2):
                ag_send(h, way, step + 1, p)

    def ag_open(h):
        for p in range(NP):
            for way in range(2):
                ag_send(h, way, 1, p)

    def w_region(core_, a_, b_, lo=0, n=6):
        return wg.at[pl.ds(((core_ * NX + a_) * NX + b_) * 6 + lo, n)]

    def b_of(q):
        return ring(b, (0, 1, -1, 2)[q], NX)

    def w_to_a(q):
        region = w_region(core, a, b_of(q))
        for way in range(2):
            send(region, region, 4, wa_sem.at[way, q], a_to[way])

    def w_to_sibling(g, q):
        region = w_region(core, ring(a, (0, 1, -1, 2)[g], NX), b_of(q))
        send(region, region, 4, wc_sem.at[0], sibling)

    def w_open():
        region = w_region(core, a, b)
        for way in range(2):
            send(region, region, 4, wb_sem.at[way], b_to[way])
        w_to_a(0)
        w_to_sibling(0, 0)

    def w_near_b():
        for way in range(2):
            q = 2 if way == 0 else 1
            landed(w_region(core, a, b_of(q)), wb_sem.at[way])
            region = w_region(core, a, b_of(q), 3 * way, 3)
            send(region, region, 4, wb_sem.at[2], b_to[way])
            w_to_a(q)
            w_to_sibling(0, q)

    def w_far_b():
        landed(w_region(core, a, b_of(3)), wb_sem.at[2])
        w_to_a(3)
        w_to_sibling(0, 3)

    def w_near_a(q):
        for way in range(2):
            g = 2 if way == 0 else 1
            a_ = ring(a, -1 if way == 0 else 1, NX)
            landed(w_region(core, a_, b_of(q)), wa_sem.at[way, q])
            region = w_region(core, a_, b_of(q), 3 * way, 3)
            send(region, region, 4, wa_sem.at[2, q], a_to[way])
            w_to_sibling(g, q)

    def w_far_a(q):
        landed(w_region(core, ring(a, 2, NX), b_of(q)), wa_sem.at[2, q])
        w_to_sibling(3, q)

    def w_close():
        landed(wg.at[pl.ds((1 - core) * DB, DB)], wc_sem.at[0])

    def plan_places():
        pltpu.make_async_copy(cols_hbm, cols, load_sem.at[4]).wait()
        pltpu.make_async_copy(cols_hbm, cols_v, load_sem.at[5]).wait()
        mine = cols_v[...]
        order = lax.broadcasted_iota(jnp.int32, (KP, DB), 0) * DB + lax.broadcasted_iota(jnp.int32, (KP, DB), 1)
        lane = lax.broadcasted_iota(jnp.int32, (8, BLK), 1)

        def body(k, carry):
            at, counts = carry
            for s in range(KP):
                col = cols[s, k]
                before = (col < mine) | ((col == mine) & (s * DB + k < order))
                at = at + jnp.where(before, 1, 0)
                counts = counts + jnp.where(lane == col, 1, 0)
            return at, counts

        at, counts = lax.fori_loop(
            0, DB, body, (jnp.zeros((KP, DB), jnp.int32), jnp.zeros((8, BLK), jnp.int32)), unroll=4
        )
        count_v[...] = counts
        copy = pltpu.make_async_copy(count_v, count, load_sem.at[6])
        copy.start()
        copy.wait()
        pair = lane
        keep = jnp.ones((8, BLK), jnp.int32)
        last = jnp.full((8, BLK), -1, jnp.int32)
        base = jnp.int32(0)
        for j in range(PB):
            n = count[0, j]
            pairs = lax.shift_right_logical(n + 1, 1)
            at = at + jnp.where(mine > j, n & 1, 0)
            keep = jnp.where(pair == base, 0, keep)
            last = last + jnp.where(lane >= j, pairs, 0)
            base = base + pairs
        place_v[...] = at
        copy = pltpu.make_async_copy(place_v, place, load_sem.at[6])
        copy.start()
        copy.wait()
        tab_v[pl.ds(8, 8)] = keep
        tab_v[pl.ds(16, 8)] = last

    def plan_table():
        slot = 2 * lax.broadcasted_iota(jnp.int32, (8, BLK), 1) + lax.broadcasted_iota(jnp.int32, (8, BLK), 0)

        def body(k, carry):
            rows, where = carry
            first = weight_position(k)
            for s in range(KP):
                hit = slot == place[s, k]
                rows = jnp.where(hit, k, rows)
                where = jnp.where(hit, first + s, where)
            return rows, where

        rows, where = lax.fori_loop(
            0, DB, body, (jnp.zeros((8, BLK), jnp.int32), jnp.full((8, BLK), ENT, jnp.int32)), unroll=2
        )
        tab_v[pl.ds(0, 8)] = rows
        tab_v[pl.ds(24, 8)] = where
        copy = pltpu.make_async_copy(tab_v, tab, load_sem.at[6])
        copy.start()
        copy.wait()

    def lanes(k):
        return pl.ds(pl.multiple_of(k * BLK, BLK), BLK)

    def fwd(h, lo, hi):
        tok = toks[h]

        def body(i, acc):
            xs = jnp.concatenate([tok[tab[TAB_K + s, i]] for s in range(2)], axis=1)
            ws = jnp.concatenate([wg[tab[TAB_W + s, i]] for s in range(2)], axis=0)
            acc = acc * tab[TAB_KEEP, i].astype(F32) + jnp.dot(xs, ws, preferred_element_type=F32)
            seg[i] = acc
            return acc

        start = jnp.zeros((T, BLK), F32) if lo == 0 else seg[lo - 1]
        lax.fori_loop(lo, hi, body, start, unroll=3)

    def gelu(h):
        rows = pl.ds(h * T, T)

        def body(j, carry):
            v = seg[tab[TAB_LAST, j]]
            k0 = 0.7978845608028654
            v2 = v * v
            th = jnp.tanh(k0 * (v + 0.044715 * (v2 * v)))
            half = 0.5 * (1.0 + th)
            slope = half + (0.5 * v) * (1.0 - th * th) * (k0 * (1.0 + 3 * 0.044715 * v2))
            act[rows, lanes(j)] = (v * half).astype(BF16)
            gps[h][j] = (cot[rows, lanes(j)].astype(F32) * slope).astype(BF16)
            return carry

        lax.fori_loop(0, PB, body, 0)
        out(act.at[rows], act_hbm.at[rows], 0)

    def grad_x(h, shard):
        gp, dx = gps[h], dxs[h]

        def body(i, carry):
            k = shard * FB + i
            at = weight_position(k)
            gs = jnp.concatenate([gp[cols[s, k]] for s in range(2)], axis=1)
            ws = jnp.concatenate([wg[at + s] for s in range(2)], axis=1)
            out = lax.dot_general(gs, ws, (((1,), (1,)), ((), ())), preferred_element_type=F32)
            dx[:, lanes(k)] = out.astype(BF16)
            return carry

        lax.fori_loop(0, FB, body, 0, unroll=3)

    def grad_w(core_, a_):
        def body(i, carry):
            b_, j = i // 3, i % 3
            at = (((core_ * NX + a_) * NX + b_) * 3 + j) * 2
            x_ = a_ + (b_ - a_) * core_
            y_ = b_ + (a_ - b_) * core_
            k = ((y_ * NX + x_) * 2 + core_) * 3 + j
            xs = jnp.concatenate([tok[k] for tok in toks], axis=0)
            picks = [cols[s, k] for s in range(2)]
            gs = jnp.concatenate(
                [jnp.concatenate([gp[col] for gp in gps], axis=0) for col in picks], axis=1
            )
            out = lax.dot_general(xs, gs, (((0,), (0,)), ((), ())), preferred_element_type=F32)
            dw[at] = out[:, :BLK].astype(BF16)
            dw[at + 1] = out[:, BLK:].astype(BF16)
            return carry

        lax.fori_loop(0, 12, body, 0, unroll=2)

    def rs_rows(way, step):
        return pl.ds(0, HALF) if step == 1 else pl.ds(HALF + (step - 2) * T, T)

    def rs_send(h, way, step, p):
        shard = ring(c, (5 - step) if way == 0 else (step - 5), NZ)
        col = pl.ds(pl.multiple_of(shard * FEAT + p * PW, PW), PW)
        rows = pl.ds(way * HALF, HALF) if step == 1 else pl.ds(0, T)
        send(
            dxs[h].at[rows, col],
            rss[h].at[way, rs_rows(way, step), pl.ds(p * PW, PW)],
            2 + h,
            rs_sem.at[h, step - 1, p],
            z_to[way],
        )

    def rs_open(h):
        for p in range(NP):
            for way in range(2):
                rs_send(h, way, 1, p)

    def rs_wait(h, step, p):
        landed(rss[h].at[:, rs_rows(0, step), pl.ds(p * PW, PW)], rs_sem.at[h, step - 1, p])

    def rs_event(h, step, p):
        dx, rs = dxs[h], rss[h]
        rs_wait(h, step, p)
        if step < 4:
            for way in range(2):
                shard = ring(c, (4 - step) if way == 0 else (step - 4), NZ)
                rows = pl.ds(way * HALF, HALF) if step == 1 else pl.ds(0, T)

                def body(i, carry):
                    at = lanes(shard * FB + p * (PW // BLK) + i)
                    got = rs[way, rs_rows(way, step), lanes(p * (PW // BLK) + i)]
                    dx[rows, at] = (dx[rows, at].astype(F32) + got.astype(F32)).astype(BF16)
                    return carry

                lax.fori_loop(0, PW // BLK, body, 0, unroll=2)
                rs_send(h, way, step + 1, p)
        else:
            def body(i, carry):
                at = lanes(c * FB + p * (PW // BLK) + i)
                total = dx[:, at].astype(F32)
                for way in range(2):
                    total += rs[way, rs_rows(way, 4), lanes(p * (PW // BLK) + i)].astype(F32)
                dx[:, at] = total.astype(BF16)
                return carry

            lax.fori_loop(0, PW // BLK, body, 0, unroll=2)
            out(
                dx.at[:, pl.ds(pl.multiple_of(c * FEAT + p * PW, PW), PW)],
                gt_hbm.at[pl.ds(h * T, T), pl.ds(p * PW, PW)],
                1,
            )

    def w_at(a_, b_=0):
        return ((core * NX + a_) * NX + b_) * 6

    def pair_send(a_):
        src = dw.at[pl.ds((((1 - core) * NX + a_) * NX) * 6, 24)]
        send(src, pr.at[pl.ds(a_ * 24, 24)], 5, gc_sem.at[a_], sibling)

    def add_blocks(dst, n, *srcs):
        def body(i, carry):
            total = dw[dst + i].astype(F32)
            for ref, at in srcs:
                total += ref[at + i].astype(F32)
            dw[dst + i] = total.astype(BF16)
            return carry

        lax.fori_loop(0, n, body, 0, unroll=2)

    def pair_add(a_):
        landed(pr.at[pl.ds(a_ * 24, 24)], gc_sem.at[a_])
        add_blocks(w_at(a_), 24, (pr, a_ * 24))

    def part(buf, way, step, size):
        off = way * (size + size // 2) + (0 if step == 0 else size // 2)
        return buf.at[pl.ds(off, size // 2 if step == 0 else size)], off

    def ring_open(buf, far, size, sems, tos):
        for way in range(2):
            dst, _ = part(buf, way, 0, size)
            send(dw.at[pl.ds(far + way * (size // 2), size // 2)], dst, 5, sems.at[way, 0], tos[way])

    def ring_middle(buf, nexts, size, sems, tos):
        for way in range(2):
            got, off = part(buf, way, 0, size)
            landed(got, sems.at[way, 0])
            add_blocks(nexts[way] + way * (size // 2), size // 2, (buf, off))
            dst, _ = part(buf, way, 1, size)
            send(dw.at[pl.ds(nexts[way], size)], dst, 5, sems.at[way, 1], tos[way])

    def ring_close(buf, own, size, sems, tos):
        srcs = []
        for way in range(2):
            got, off = part(buf, way, 1, size)
            landed(got, sems.at[way, 1])
            srcs.append((buf, off))
        add_blocks(own, size, *srcs)

    a_near = (w_at(ring(a, 1, NX)), w_at(ring(a, -1, NX)))
    b_near = (w_at(a, ring(b, 1, NX)), w_at(a, ring(b, -1, NX)))

    wg[ENT] = jnp.zeros((BLK, BLK), BF16)
    tok_wait(0)
    ag_open(0)
    w_load.wait()
    w_open()
    tok_load(1)
    cot_load.start()
    ag_event(0, 1, 0)
    w_near_b()
    w_near_a(0)
    ag_event(0, 1, 1)
    w_far_b()
    ag_event(0, 2, 0)
    w_near_a(1)
    w_near_a(2)
    ag_event(0, 2, 1)
    w_near_a(3)
    w_far_a(0)
    ag_event(0, 3, 0)
    w_far_a(1)
    w_far_a(2)
    w_far_a(3)
    tok_wait(1)
    ag_event(0, 3, 1)
    ag_open(1)
    plan_places()
    plan_table()
    cot_load.wait()
    w_close()
    ag_event(0, 4, 0)
    ag_event(0, 4, 1)

    quarter = PAIRS // 4
    fwd(0, 0, quarter)
    ag_event(1, 1, 0)
    fwd(0, quarter, 2 * quarter)
    ag_event(1, 1, 1)
    fwd(0, 2 * quarter, 3 * quarter)
    fwd(0, 3 * quarter, PAIRS)
    ag_event(1, 2, 0)
    gelu(0)
    grad_x(0, ring(c, 4, NZ))
    ag_event(1, 2, 1)
    grad_x(0, ring(c, 3, NZ))
    grad_x(0, ring(c, -3, NZ))
    grad_x(0, ring(c, 2, NZ))
    ag_event(1, 3, 0)
    grad_x(0, ring(c, -2, NZ))
    grad_x(0, ring(c, 1, NZ))
    grad_x(0, ring(c, -1, NZ))
    grad_x(0, c)
    ag_event(1, 3, 1)
    rs_open(0)
    ag_event(1, 4, 0)
    ag_event(1, 4, 1)

    fwd(1, 0, quarter)
    rs_event(0, 1, 0)
    fwd(1, quarter, 2 * quarter)
    rs_event(0, 1, 1)
    fwd(1, 2 * quarter, 3 * quarter)
    fwd(1, 3 * quarter, PAIRS)
    gelu(1)
    rs_event(0, 2, 0)
    for g in range(2):
        grad_w(1 - core, g)
        pair_send(g)
    rs_event(0, 2, 1)
    for g in range(2, 4):
        grad_w(1 - core, g)
        pair_send(g)
    grad_w(core, ring(a, 2, NX))
    rs_event(0, 3, 0)
    grad_x(1, ring(c, 4, NZ))
    rs_open(1)
    pair_add(ring(a, 2, NX))
    ring_open(bufa, w_at(ring(a, 2, NX)), 24, ga_sem, a_to)
    grad_w(core, ring(a, 1, NX))
    grad_w(core, ring(a, -1, NX))
    rs_event(0, 3, 1)
    grad_x(1, ring(c, 3, NZ))
    grad_x(1, ring(c, -3, NZ))
    pair_add(ring(a, 1, NX))
    pair_add(ring(a, -1, NX))
    ring_middle(bufa, a_near, 24, ga_sem, a_to)
    rs_event(1, 1, 0)
    grad_w(core, a)
    pair_add(a)
    rs_event(0, 4, 0)
    grad_x(1, ring(c, 2, NZ))
    grad_x(1, ring(c, -2, NZ))
    rs_event(1, 1, 1)
    rs_event(0, 4, 1)
    grad_x(1, ring(c, 1, NZ))
    grad_x(1, ring(c, -1, NZ))
    grad_x(1, c)
    rs_event(1, 2, 0)
    ring_close(bufa, w_at(a), 24, ga_sem, a_to)
    ring_open(bufb, w_at(a, ring(b, 2, NX)), 6, gb_sem, b_to)
    rs_event(1, 2, 1)
    ring_middle(bufb, b_near, 6, gb_sem, b_to)
    rs_event(1, 3, 0)
    ring_close(bufb, w_at(a, b), 6, gb_sem, b_to)
    out(dw.at[pl.ds(w_at(a, b), 6)], gb_hbm, 2)
    rs_event(1, 3, 1)
    pltpu.make_async_copy(act, act_hbm, out_sem.at[0]).wait()
    for h in range(CHUNKS):
        landed(toks[h].at[pl.ds(0, 7 * FB)], send_sem.at[h])
    landed(dx0.at[:, pl.ds(0, 7 * FEAT)], send_sem.at[2])
    landed(wg.at[pl.ds(0, 31 * 6)], send_sem.at[4])
    landed(dw.at[pl.ds(0, 31 * 6)], send_sem.at[5])
    pltpu.make_async_copy(dw.at[pl.ds(0, 6)], gb_hbm, out_sem.at[2]).wait()
    rs_event(1, 4, 0)
    rs_event(1, 4, 1)

    landed(dx1.at[:, pl.ds(0, 7 * FEAT)], send_sem.at[3])
    pltpu.make_async_copy(dx0.at[:, pl.ds(0, CHUNKS * FEAT)], dx1.at[:, pl.ds(0, CHUNKS * FEAT)], out_sem.at[1]).wait()


def finish(act, gt, gb, act_out, gt_out, gb_out, sem_out):
    parts = [(act, act_out, pl.ds(i * 64, 64)) for i in range(4)]
    parts += [(gt, gt_out, pl.ds(i * 128, 128)) for i in range(2)]
    parts += [(gb, gb_out, pl.ds(0, 6))]
    stores = [pltpu.make_async_copy(mid.at[at], dst.at[at], sem_out.at[i]) for i, (mid, dst, at) in enumerate(parts)]
    for copy in stores:
        copy.start()
    for copy in stores:
        copy.wait()


def on_device(tokens, weight_blocks, block_cols, cotangent):
    any_space = pl.BlockSpec(memory_space=pl.ANY)
    hbm = pl.BlockSpec(memory_space=pltpu.HBM)
    arrays = (block_cols.T, tokens, weight_blocks.reshape(6, BLK, BLK), cotangent)
    in_hbm = [pltpu.with_memory_space_constraint(v, pltpu.HBM) for v in arrays]
    dma = pltpu.SemaphoreType.DMA
    act, grad_tokens, grad_blocks = pl.pallas_call(
        kernel,
        out_shape=(
            jax.ShapeDtypeStruct((CHUNKS * T, PB * BLK), BF16),
            jax.ShapeDtypeStruct((CHUNKS * T, FEAT), BF16),
            jax.ShapeDtypeStruct((6, BLK, BLK), BF16),
        ),
        in_specs=[hbm] * 4,
        out_specs=(any_space, any_space, any_space),
        scratch_shapes=[
            pltpu.VMEM((DB, T, BLK), BF16),
            pltpu.VMEM((DB, T, BLK), BF16),
            pltpu.VMEM((ENT + 1, BLK, BLK), BF16),
            pltpu.VMEM((PAIRS, T, BLK), F32),
            pltpu.VMEM((CHUNKS * T, PB * BLK), BF16),
            pltpu.VMEM((CHUNKS * T, PB * BLK), BF16),
            pltpu.VMEM((PB, T, BLK), BF16),
            pltpu.VMEM((PB, T, BLK), BF16),
            pltpu.VMEM((T, DB * BLK), BF16),
            pltpu.VMEM((T, DB * BLK), BF16),
            pltpu.VMEM((2, HALF + 3 * T, FEAT), BF16),
            pltpu.VMEM((2, HALF + 3 * T, FEAT), BF16),
            pltpu.VMEM((ENT, BLK, BLK), BF16),
            pltpu.VMEM((ENT // 2, BLK, BLK), BF16),
            pltpu.VMEM((2 * 36, BLK, BLK), BF16),
            pltpu.VMEM((2 * 9, BLK, BLK), BF16),
            pltpu.VMEM((KP, DB), jnp.int32),
            pltpu.SMEM((KP, DB), jnp.int32),
            pltpu.VMEM((8, BLK), jnp.int32),
            pltpu.SMEM((8, BLK), jnp.int32),
            pltpu.VMEM((KP, DB), jnp.int32),
            pltpu.SMEM((KP, DB), jnp.int32),
            pltpu.VMEM((32, BLK), jnp.int32),
            pltpu.SMEM((32, BLK), jnp.int32),
            dma((7,)),
            dma((3,)),
            dma((6,)),
            dma((CHUNKS, 4, NP)),
            dma((CHUNKS, 4, NP)),
            dma((3,)),
            dma((3, 4)),
            dma((1,)),
            dma((4,)),
            dma((2, 2)),
            dma((2, 2)),
        ],
        compiler_params=pltpu.CompilerParams(
            collective_id=0, has_side_effects=True, vmem_limit_bytes=50 * 1024 * 1024
        ),
        cost_estimate=pl.CostEstimate(flops=4_831_838_208, bytes_accessed=6_000_000, transcendentals=786_432),
    )(*in_hbm)
    act, grad_tokens, grad_blocks = pl.pallas_call(
        finish,
        out_shape=tuple(jax.ShapeDtypeStruct(v.shape, v.dtype) for v in (act, grad_tokens, grad_blocks)),
        in_specs=[any_space] * 3,
        out_specs=(hbm,) * 3,
        scratch_shapes=[dma((7,))],
        compiler_params=pltpu.CompilerParams(vmem_limit_bytes=1024 * 1024),
    )(act, grad_tokens, grad_blocks)
    return act, grad_tokens, grad_blocks.reshape(3, KP, BLK, BLK)


def solution(mesh):
    return jax.shard_map(
        on_device,
        mesh=mesh,
        in_specs=(P("row", "col"), P("row", "col", None, None), P(None, "col"), P("row", "col")),
        out_specs=(P("row", "col"), P("row", "col"), P("row", "col", None, None)),
        check_vma=False,
    )
```

```python
import jax
import jax.numpy as jnp
from jax import lax
from jax.experimental import pallas as pl
from jax.experimental.pallas import tpu as pltpu
from jax.sharding import PartitionSpec as P

MESH = pl.DeviceIdType.MESH
F32 = jnp.float32
BF16 = jnp.bfloat16

BLK = 128
PB = 24
KP = 2
DB = 96
NX = 4
NZ = 8
ENT = DB * KP
PAIRS = (ENT + PB) // 2
CHUNKS = 2
T = 128
FEAT = 1536
FB = FEAT // BLK
NP = 2
PW = FEAT // NP
HALF = T // 2

TAB_K, TAB_KEEP, TAB_LAST, TAB_W = 0, 8, 16, 24


def weight_position(k):
    r, i = k // 3, k % 3
    core = r % 2
    x = (r // 2) % NX
    y = r // (2 * NX)
    a = x + (y - x) * core
    b = y + (x - y) * core
    return (((core * NX + a) * NX + b) * 3 + i) * 2


def kernel(
    cols_hbm, tok_hbm, w_hbm, cot_hbm,
    act, gt, gb,
    tok0, tok1, wg, seg, cot, gp0, gp1, dx0, dx1, rs0, rs1, dw, pr, bufa, bufb,
    cols_v, cols, count_v, count, place_v, place, tab_v, tab,
    load_sem, out_sem, send_sem, ag_sem, rs_sem, wb_sem, wa_sem, wc_sem, gc_sem, ga_sem, gb_sem,
):
    toks, gps, dxs, rss = (tok0, tok1), (gp0, gp1), (dx0, dx1), (rs0, rs1)
    row, c = lax.axis_index("row"), lax.axis_index("col")
    core = row % 2
    x = (row // 2) % NX
    y = row // (2 * NX)
    a = x + (y - x) * core
    b = y + (x - y) * core

    def ring(v, step, n):
        return lax.rem(v + step + n, n)

    def chip(a_, b_):
        x_ = a_ + (b_ - a_) * core
        y_ = b_ + (a_ - b_) * core
        return ((y_ * NX + x_) * 2 + core, c)

    z_to = ((row, ring(c, 1, NZ)), (row, ring(c, -1, NZ)))
    a_to = (chip(ring(a, 1, NX), b), chip(ring(a, -1, NX), b))
    b_to = (chip(a, ring(b, 1, NX)), chip(a, ring(b, -1, NX)))
    sibling = (row + 1 - 2 * core, c)

    def remote(src, dst, sends, recv, to):
        return pltpu.make_async_remote_copy(
            src_ref=src, dst_ref=dst, send_sem=send_sem.at[sends], recv_sem=recv, device_id=to, device_id_type=MESH
        )

    def send(src, dst, sends, recv, to):
        remote(src, dst, sends, recv, to).start()

    def landed(region, recv):
        pltpu.make_async_copy(region, region, recv).wait()

    def out(src, dst, at):
        pltpu.make_async_copy(src, dst, out_sem.at[at]).start()

    w_load = pltpu.make_async_copy(w_hbm, wg.at[pl.ds(((core * NX + a) * NX + b) * 6, 6)], load_sem.at[2])
    cot_load = pltpu.make_async_copy(cot_hbm, cot, load_sem.at[3])

    def tok_load(h):
        for i in range(FB):
            pltpu.make_async_copy(
                tok_hbm.at[pl.ds(h * T, T), pl.ds(i * BLK, BLK)], toks[h].at[c * FB + i], load_sem.at[h]
            ).start()

    def tok_wait(h):
        region = toks[h].at[pl.ds(c * FB, FB)]
        pltpu.make_async_copy(region, region, load_sem.at[h]).wait()

    barrier = pltpu.get_barrier_semaphore()
    for to in (*z_to, *a_to, *b_to, sibling):
        pl.semaphore_signal(barrier, inc=1, device_id=to, device_id_type=MESH)
    tok_load(0)
    w_load.start()
    pltpu.make_async_copy(cols_hbm, cols, load_sem.at[4]).start()
    pltpu.make_async_copy(cols_hbm, cols_v, load_sem.at[5]).start()
    pl.semaphore_wait(barrier, 7)

    def ag_region(h, shard, way, step, p):
        rows = pl.ds(0, T) if step < 4 else pl.ds(way * HALF, HALF)
        return toks[h].at[pl.ds(shard * FB + p * (FB // NP), FB // NP), rows]

    def ag_send(h, way, step, p):
        shard = ring(c, (1 - step) if way == 0 else (step - 1), NZ)
        region = ag_region(h, shard, way, step, p)
        send(region, region, h, ag_sem.at[h, step - 1, p], z_to[way])

    def ag_event(h, step, p):
        n = FB // NP if step == 4 else 2 * FB // NP
        landed(toks[h].at[pl.ds(0, n)], ag_sem.at[h, step - 1, p])
        if step < 4:
            for way in range(2):
                ag_send(h, way, step + 1, p)

    def ag_open(h):
        for p in range(NP):
            for way in range(2):
                ag_send(h, way, 1, p)

    def w_region(core_, a_, b_, lo=0, n=6):
        return wg.at[pl.ds(((core_ * NX + a_) * NX + b_) * 6 + lo, n)]

    def b_of(q):
        return ring(b, (0, 1, -1, 2)[q], NX)

    def w_to_a(q):
        region = w_region(core, a, b_of(q))
        for way in range(2):
            send(region, region, 4, wa_sem.at[way, q], a_to[way])

    def w_to_sibling(g, q):
        region = w_region(core, ring(a, (0, 1, -1, 2)[g], NX), b_of(q))
        send(region, region, 4, wc_sem.at[0], sibling)

    def w_open():
        region = w_region(core, a, b)
        for way in range(2):
            send(region, region, 4, wb_sem.at[way], b_to[way])
        w_to_a(0)
        w_to_sibling(0, 0)

    def w_near_b():
        for way in range(2):
            q = 2 if way == 0 else 1
            landed(w_region(core, a, b_of(q)), wb_sem.at[way])
            region = w_region(core, a, b_of(q), 3 * way, 3)
            send(region, region, 4, wb_sem.at[2], b_to[way])
            w_to_a(q)
            w_to_sibling(0, q)

    def w_far_b():
        landed(w_region(core, a, b_of(3)), wb_sem.at[2])
        w_to_a(3)
        w_to_sibling(0, 3)

    def w_near_a(q):
        for way in range(2):
            g = 2 if way == 0 else 1
            a_ = ring(a, -1 if way == 0 else 1, NX)
            landed(w_region(core, a_, b_of(q)), wa_sem.at[way, q])
            region = w_region(core, a_, b_of(q), 3 * way, 3)
            send(region, region, 4, wa_sem.at[2, q], a_to[way])
            w_to_sibling(g, q)

    def w_far_a(q):
        landed(w_region(core, ring(a, 2, NX), b_of(q)), wa_sem.at[2, q])
        w_to_sibling(3, q)

    def w_close():
        landed(wg.at[pl.ds((1 - core) * DB, DB)], wc_sem.at[0])

    def plan_places():
        pltpu.make_async_copy(cols_hbm, cols, load_sem.at[4]).wait()
        pltpu.make_async_copy(cols_hbm, cols_v, load_sem.at[5]).wait()
        mine = cols_v[...]
        order = lax.broadcasted_iota(jnp.int32, (KP, DB), 0) * DB + lax.broadcasted_iota(jnp.int32, (KP, DB), 1)
        lane = lax.broadcasted_iota(jnp.int32, (8, BLK), 1)

        def body(k, carry):
            at, counts = carry
            for s in range(KP):
                col = cols[s, k]
                before = (col < mine) | ((col == mine) & (s * DB + k < order))
                at = at + jnp.where(before, 1, 0)
                counts = counts + jnp.where(lane == col, 1, 0)
            return at, counts

        at, counts = lax.fori_loop(
            0, DB, body, (jnp.zeros((KP, DB), jnp.int32), jnp.zeros((8, BLK), jnp.int32)), unroll=4
        )
        count_v[...] = counts
        copy = pltpu.make_async_copy(count_v, count, load_sem.at[6])
        copy.start()
        copy.wait()
        pair = lane
        keep = jnp.ones((8, BLK), jnp.int32)
        last = jnp.full((8, BLK), -1, jnp.int32)
        base = jnp.int32(0)
        for j in range(PB):
            n = count[0, j]
            pairs = lax.shift_right_logical(n + 1, 1)
            at = at + jnp.where(mine > j, n & 1, 0)
            keep = jnp.where(pair == base, 0, keep)
            last = last + jnp.where(lane >= j, pairs, 0)
            base = base + pairs
        place_v[...] = at
        copy = pltpu.make_async_copy(place_v, place, load_sem.at[6])
        copy.start()
        copy.wait()
        tab_v[pl.ds(8, 8)] = keep
        tab_v[pl.ds(16, 8)] = last

    def plan_table():
        slot = 2 * lax.broadcasted_iota(jnp.int32, (8, BLK), 1) + lax.broadcasted_iota(jnp.int32, (8, BLK), 0)

        def body(k, carry):
            rows, where = carry
            first = weight_position(k)
            for s in range(KP):
                hit = slot == place[s, k]
                rows = jnp.where(hit, k, rows)
                where = jnp.where(hit, first + s, where)
            return rows, where

        rows, where = lax.fori_loop(
            0, DB, body, (jnp.zeros((8, BLK), jnp.int32), jnp.full((8, BLK), ENT, jnp.int32)), unroll=2
        )
        tab_v[pl.ds(0, 8)] = rows
        tab_v[pl.ds(24, 8)] = where
        copy = pltpu.make_async_copy(tab_v, tab, load_sem.at[6])
        copy.start()
        copy.wait()

    def lanes(k):
        return pl.ds(pl.multiple_of(k * BLK, BLK), BLK)

    def fwd(h, lo, hi):
        tok = toks[h]

        def body(i, acc):
            xs = jnp.concatenate([tok[tab[TAB_K + s, i]] for s in range(2)], axis=1)
            ws = jnp.concatenate([wg[tab[TAB_W + s, i]] for s in range(2)], axis=0)
            acc = acc * tab[TAB_KEEP, i].astype(F32) + jnp.dot(xs, ws, preferred_element_type=F32)
            seg[i] = acc
            return acc

        start = jnp.zeros((T, BLK), F32) if lo == 0 else seg[lo - 1]
        lax.fori_loop(lo, hi, body, start, unroll=3)

    def gelu(h):
        rows = pl.ds(h * T, T)

        def body(j, carry):
            v = seg[tab[TAB_LAST, j]]
            k0 = 0.7978845608028654
            v2 = v * v
            th = jnp.tanh(k0 * (v + 0.044715 * (v2 * v)))
            half = 0.5 * (1.0 + th)
            slope = half + (0.5 * v) * (1.0 - th * th) * (k0 * (1.0 + 3 * 0.044715 * v2))
            act[rows, lanes(j)] = (v * half).astype(BF16)
            gps[h][j] = (cot[rows, lanes(j)].astype(F32) * slope).astype(BF16)
            return carry

        lax.fori_loop(0, PB, body, 0)

    def grad_x(h, shard):
        gp, dx = gps[h], dxs[h]

        def body(i, carry):
            k = shard * FB + i
            at = weight_position(k)
            gs = jnp.concatenate([gp[cols[s, k]] for s in range(2)], axis=1)
            ws = jnp.concatenate([wg[at + s] for s in range(2)], axis=1)
            out = lax.dot_general(gs, ws, (((1,), (1,)), ((), ())), preferred_element_type=F32)
            dx[:, lanes(k)] = out.astype(BF16)
            return carry

        lax.fori_loop(0, FB, body, 0, unroll=3)

    def grad_w(core_, a_):
        def body(i, carry):
            b_, j = i // 3, i % 3
            at = (((core_ * NX + a_) * NX + b_) * 3 + j) * 2
            x_ = a_ + (b_ - a_) * core_
            y_ = b_ + (a_ - b_) * core_
            k = ((y_ * NX + x_) * 2 + core_) * 3 + j
            xs = jnp.concatenate([tok[k] for tok in toks], axis=0)
            picks = [cols[s, k] for s in range(2)]
            gs = jnp.concatenate(
                [jnp.concatenate([gp[col] for gp in gps], axis=0) for col in picks], axis=1
            )
            out = lax.dot_general(xs, gs, (((0,), (0,)), ((), ())), preferred_element_type=F32)
            dw[at] = out[:, :BLK].astype(BF16)
            dw[at + 1] = out[:, BLK:].astype(BF16)
            return carry

        lax.fori_loop(0, 12, body, 0, unroll=2)

    def rs_rows(way, step):
        return pl.ds(0, HALF) if step == 1 else pl.ds(HALF + (step - 2) * T, T)

    def rs_send(h, way, step, p):
        shard = ring(c, (5 - step) if way == 0 else (step - 5), NZ)
        col = pl.ds(pl.multiple_of(shard * FEAT + p * PW, PW), PW)
        rows = pl.ds(way * HALF, HALF) if step == 1 else pl.ds(0, T)
        send(
            dxs[h].at[rows, col],
            rss[h].at[way, rs_rows(way, step), pl.ds(p * PW, PW)],
            2 + h,
            rs_sem.at[h, step - 1, p],
            z_to[way],
        )

    def rs_open(h):
        for p in range(NP):
            for way in range(2):
                rs_send(h, way, 1, p)

    def rs_wait(h, step, p):
        landed(rss[h].at[:, rs_rows(0, step), pl.ds(p * PW, PW)], rs_sem.at[h, step - 1, p])

    def rs_event(h, step, p):
        dx, rs = dxs[h], rss[h]
        rs_wait(h, step, p)
        if step < 4:
            for way in range(2):
                shard = ring(c, (4 - step) if way == 0 else (step - 4), NZ)
                rows = pl.ds(way * HALF, HALF) if step == 1 else pl.ds(0, T)

                def body(i, carry):
                    at = lanes(shard * FB + p * (PW // BLK) + i)
                    got = rs[way, rs_rows(way, step), lanes(p * (PW // BLK) + i)]
                    dx[rows, at] = (dx[rows, at].astype(F32) + got.astype(F32)).astype(BF16)
                    return carry

                lax.fori_loop(0, PW // BLK, body, 0, unroll=2)
                rs_send(h, way, step + 1, p)
        else:
            def body(i, carry):
                at = lanes(c * FB + p * (PW // BLK) + i)
                total = dx[:, at].astype(F32)
                for way in range(2):
                    total += rs[way, rs_rows(way, 4), lanes(p * (PW // BLK) + i)].astype(F32)
                gt[pl.ds(h * T, T), lanes(p * (PW // BLK) + i)] = total.astype(BF16)
                return carry

            lax.fori_loop(0, PW // BLK, body, 0, unroll=2)

    def w_at(a_, b_=0):
        return ((core * NX + a_) * NX + b_) * 6

    def pair_send(a_):
        src = dw.at[pl.ds((((1 - core) * NX + a_) * NX) * 6, 24)]
        send(src, pr.at[pl.ds(a_ * 24, 24)], 5, gc_sem.at[a_], sibling)

    def add_blocks(dst, n, *srcs):
        def body(i, carry):
            total = dw[dst + i].astype(F32)
            for ref, at in srcs:
                total += ref[at + i].astype(F32)
            dw[dst + i] = total.astype(BF16)
            return carry

        lax.fori_loop(0, n, body, 0, unroll=2)

    def pair_add(a_):
        landed(pr.at[pl.ds(a_ * 24, 24)], gc_sem.at[a_])
        add_blocks(w_at(a_), 24, (pr, a_ * 24))

    def part(buf, way, step, size):
        off = way * (size + size // 2) + (0 if step == 0 else size // 2)
        return buf.at[pl.ds(off, size // 2 if step == 0 else size)], off

    def ring_open(buf, far, size, sems, tos):
        for way in range(2):
            dst, _ = part(buf, way, 0, size)
            send(dw.at[pl.ds(far + way * (size // 2), size // 2)], dst, 5, sems.at[way, 0], tos[way])

    def ring_middle(buf, nexts, size, sems, tos):
        for way in range(2):
            got, off = part(buf, way, 0, size)
            landed(got, sems.at[way, 0])
            add_blocks(nexts[way] + way * (size // 2), size // 2, (buf, off))
            dst, _ = part(buf, way, 1, size)
            send(dw.at[pl.ds(nexts[way], size)], dst, 5, sems.at[way, 1], tos[way])

    def ring_close(buf, own, size, sems, tos):
        srcs = []
        for way in range(2):
            got, off = part(buf, way, 1, size)
            landed(got, sems.at[way, 1])
            srcs.append((buf, off))
        add_blocks(own, size, *srcs)

    a_near = (w_at(ring(a, 1, NX)), w_at(ring(a, -1, NX)))
    b_near = (w_at(a, ring(b, 1, NX)), w_at(a, ring(b, -1, NX)))

    wg[ENT] = jnp.zeros((BLK, BLK), BF16)
    tok_wait(0)
    ag_open(0)
    w_load.wait()
    w_open()
    tok_load(1)
    cot_load.start()
    ag_event(0, 1, 0)
    w_near_b()
    w_near_a(0)
    ag_event(0, 1, 1)
    w_far_b()
    ag_event(0, 2, 0)
    w_near_a(1)
    w_near_a(2)
    ag_event(0, 2, 1)
    w_near_a(3)
    w_far_a(0)
    ag_event(0, 3, 0)
    w_far_a(1)
    w_far_a(2)
    w_far_a(3)
    tok_wait(1)
    ag_event(0, 3, 1)
    ag_open(1)
    plan_places()
    plan_table()
    cot_load.wait()
    w_close()
    ag_event(0, 4, 0)
    ag_event(0, 4, 1)

    quarter = PAIRS // 4
    fwd(0, 0, quarter)
    ag_event(1, 1, 0)
    fwd(0, quarter, 2 * quarter)
    ag_event(1, 1, 1)
    fwd(0, 2 * quarter, 3 * quarter)
    fwd(0, 3 * quarter, PAIRS)
    ag_event(1, 2, 0)
    gelu(0)
    grad_x(0, ring(c, 4, NZ))
    ag_event(1, 2, 1)
    grad_x(0, ring(c, 3, NZ))
    grad_x(0, ring(c, -3, NZ))
    grad_x(0, ring(c, 2, NZ))
    ag_event(1, 3, 0)
    grad_x(0, ring(c, -2, NZ))
    grad_x(0, ring(c, 1, NZ))
    grad_x(0, ring(c, -1, NZ))
    grad_x(0, c)
    ag_event(1, 3, 1)
    rs_open(0)
    ag_event(1, 4, 0)
    ag_event(1, 4, 1)

    fwd(1, 0, quarter)
    rs_event(0, 1, 0)
    fwd(1, quarter, 2 * quarter)
    rs_event(0, 1, 1)
    fwd(1, 2 * quarter, 3 * quarter)
    fwd(1, 3 * quarter, PAIRS)
    gelu(1)
    rs_event(0, 2, 0)
    for g in range(2):
        grad_w(1 - core, g)
        pair_send(g)
    rs_event(0, 2, 1)
    for g in range(2, 4):
        grad_w(1 - core, g)
        pair_send(g)
    grad_w(core, ring(a, 2, NX))
    rs_event(0, 3, 0)
    grad_x(1, ring(c, 4, NZ))
    rs_open(1)
    pair_add(ring(a, 2, NX))
    ring_open(bufa, w_at(ring(a, 2, NX)), 24, ga_sem, a_to)
    grad_w(core, ring(a, 1, NX))
    grad_w(core, ring(a, -1, NX))
    rs_event(0, 3, 1)
    grad_x(1, ring(c, 3, NZ))
    grad_x(1, ring(c, -3, NZ))
    pair_add(ring(a, 1, NX))
    pair_add(ring(a, -1, NX))
    ring_middle(bufa, a_near, 24, ga_sem, a_to)
    rs_event(1, 1, 0)
    grad_w(core, a)
    pair_add(a)
    rs_event(0, 4, 0)
    grad_x(1, ring(c, 2, NZ))
    grad_x(1, ring(c, -2, NZ))
    rs_event(1, 1, 1)
    rs_event(0, 4, 1)
    grad_x(1, ring(c, 1, NZ))
    grad_x(1, ring(c, -1, NZ))
    grad_x(1, c)
    rs_event(1, 2, 0)
    ring_close(bufa, w_at(a), 24, ga_sem, a_to)
    ring_open(bufb, w_at(a, ring(b, 2, NX)), 6, gb_sem, b_to)
    rs_event(1, 2, 1)
    ring_middle(bufb, b_near, 6, gb_sem, b_to)
    rs_event(1, 3, 0)
    ring_close(bufb, w_at(a, b), 6, gb_sem, b_to)
    out(dw.at[pl.ds(w_at(a, b), 6)], gb, 0)
    rs_event(1, 3, 1)
    for h in range(CHUNKS):
        landed(toks[h].at[pl.ds(0, 7 * FB)], send_sem.at[h])
    landed(dx0.at[:, pl.ds(0, 7 * FEAT)], send_sem.at[2])
    landed(wg.at[pl.ds(0, 31 * 6)], send_sem.at[4])
    landed(dw.at[pl.ds(0, 31 * 6)], send_sem.at[5])
    pltpu.make_async_copy(dw.at[pl.ds(0, 6)], gb, out_sem.at[0]).wait()
    rs_event(1, 4, 0)
    rs_event(1, 4, 1)

    landed(dx1.at[:, pl.ds(0, 7 * FEAT)], send_sem.at[3])


def finish(act, gt, gb, act_out, gt_out, gb_out, sem_out):
    parts = [(act, act_out, pl.ds(i * 64, 64)) for i in range(4)]
    parts += [(gt, gt_out, pl.ds(i * 128, 128)) for i in range(2)]
    parts += [(gb, gb_out, pl.ds(0, 6))]
    stores = [pltpu.make_async_copy(mid.at[at], dst.at[at], sem_out.at[i]) for i, (mid, dst, at) in enumerate(parts)]
    for copy in stores:
        copy.start()
    for copy in stores:
        copy.wait()


def on_device(tokens, weight_blocks, block_cols, cotangent):
    hbm = pl.BlockSpec(memory_space=pltpu.HBM)
    arrays = (block_cols.T, tokens, weight_blocks.reshape(6, BLK, BLK), cotangent)
    in_hbm = [pltpu.with_memory_space_constraint(v, pltpu.HBM) for v in arrays]
    dma = pltpu.SemaphoreType.DMA
    act, grad_tokens, grad_blocks = pl.pallas_call(
        kernel,
        out_shape=(
            jax.ShapeDtypeStruct((CHUNKS * T, PB * BLK), BF16),
            jax.ShapeDtypeStruct((CHUNKS * T, FEAT), BF16),
            jax.ShapeDtypeStruct((6, BLK, BLK), BF16),
        ),
        in_specs=[hbm] * 4,
        out_specs=(pl.BlockSpec(memory_space=pltpu.VMEM),) * 3,
        scratch_shapes=[
            pltpu.VMEM((DB, T, BLK), BF16),
            pltpu.VMEM((DB, T, BLK), BF16),
            pltpu.VMEM((ENT + 1, BLK, BLK), BF16),
            pltpu.VMEM((PAIRS, T, BLK), F32),
            pltpu.VMEM((CHUNKS * T, PB * BLK), BF16),
            pltpu.VMEM((PB, T, BLK), BF16),
            pltpu.VMEM((PB, T, BLK), BF16),
            pltpu.VMEM((T, DB * BLK), BF16),
            pltpu.VMEM((T, DB * BLK), BF16),
            pltpu.VMEM((2, HALF + 3 * T, FEAT), BF16),
            pltpu.VMEM((2, HALF + 3 * T, FEAT), BF16),
            pltpu.VMEM((ENT, BLK, BLK), BF16),
            pltpu.VMEM((ENT // 2, BLK, BLK), BF16),
            pltpu.VMEM((2 * 36, BLK, BLK), BF16),
            pltpu.VMEM((2 * 9, BLK, BLK), BF16),
            pltpu.VMEM((KP, DB), jnp.int32),
            pltpu.SMEM((KP, DB), jnp.int32),
            pltpu.VMEM((8, BLK), jnp.int32),
            pltpu.SMEM((8, BLK), jnp.int32),
            pltpu.VMEM((KP, DB), jnp.int32),
            pltpu.SMEM((KP, DB), jnp.int32),
            pltpu.VMEM((32, BLK), jnp.int32),
            pltpu.SMEM((32, BLK), jnp.int32),
            dma((7,)),
            dma((1,)),
            dma((6,)),
            dma((CHUNKS, 4, NP)),
            dma((CHUNKS, 4, NP)),
            dma((3,)),
            dma((3, 4)),
            dma((1,)),
            dma((4,)),
            dma((2, 2)),
            dma((2, 2)),
        ],
        compiler_params=pltpu.CompilerParams(
            collective_id=0, has_side_effects=True, vmem_limit_bytes=50 * 1024 * 1024
        ),
        cost_estimate=pl.CostEstimate(flops=4_831_838_208, bytes_accessed=6_000_000, transcendentals=786_432),
    )(*in_hbm)
    act, grad_tokens, grad_blocks = pl.pallas_call(
        finish,
        out_shape=tuple(jax.ShapeDtypeStruct(v.shape, v.dtype) for v in (act, grad_tokens, grad_blocks)),
        in_specs=[pl.BlockSpec(memory_space=pltpu.VMEM)] * 3,
        out_specs=(hbm,) * 3,
        scratch_shapes=[dma((7,))],
        compiler_params=pltpu.CompilerParams(vmem_limit_bytes=4 * 1024 * 1024),
    )(act, grad_tokens, grad_blocks)
    return act, grad_tokens, grad_blocks.reshape(3, KP, BLK, BLK)


def solution(mesh):
    return jax.shard_map(
        on_device,
        mesh=mesh,
        in_specs=(P("row", "col"), P("row", "col", None, None), P(None, "col"), P("row", "col")),
        out_specs=(P("row", "col"), P("row", "col"), P("row", "col", None, None)),
        check_vma=False,
    )
```

```python
import jax
import jax.numpy as jnp
from jax import lax
from jax.experimental import pallas as pl
from jax.experimental.pallas import tpu as pltpu
from jax.sharding import PartitionSpec as P

MESH = pl.DeviceIdType.MESH
F32 = jnp.float32
BF16 = jnp.bfloat16

BLK = 128
PB = 24
KP = 2
DB = 96
NX = 4
NZ = 8
ENT = DB * KP
PAIRS = (ENT + PB) // 2
CHUNKS = 2
T = 128
FEAT = 1536
FB = FEAT // BLK
NP = 2
PW = FEAT // NP
HALF = T // 2

TAB_K, TAB_KEEP, TAB_LAST, TAB_W = 0, 8, 16, 24


def weight_position(k):
    r, i = k // 3, k % 3
    core = r % 2
    x = (r // 2) % NX
    y = r // (2 * NX)
    a = x + (y - x) * core
    b = y + (x - y) * core
    return (((core * NX + a) * NX + b) * 3 + i) * 2


def kernel(
    cols_hbm, tok_hbm, w_hbm, cot_hbm,
    act, gt, gb,
    tok0, tok1, wg, seg, cot, gp0, gp1, dx0, dx1, rs0, rs1, dw, pr, bufa, bufb,
    cols_v, cols, count_v, count, place_v, place, tab_v, tab,
    load_sem, out_sem, send_sem, ag_sem, rs_sem, wb_sem, wa_sem, wc_sem, gc_sem, ga_sem, gb_sem,
):
    toks, gps, dxs, rss = (tok0, tok1), (gp0, gp1), (dx0, dx1), (rs0, rs1)
    row, c = lax.axis_index("row"), lax.axis_index("col")
    core = row % 2
    x = (row // 2) % NX
    y = row // (2 * NX)
    a = x + (y - x) * core
    b = y + (x - y) * core

    def ring(v, step, n):
        return lax.rem(v + step + n, n)

    def chip(a_, b_):
        x_ = a_ + (b_ - a_) * core
        y_ = b_ + (a_ - b_) * core
        return ((y_ * NX + x_) * 2 + core, c)

    z_to = ((row, ring(c, 1, NZ)), (row, ring(c, -1, NZ)))
    a_to = (chip(ring(a, 1, NX), b), chip(ring(a, -1, NX), b))
    b_to = (chip(a, ring(b, 1, NX)), chip(a, ring(b, -1, NX)))
    sibling = (row + 1 - 2 * core, c)

    def remote(src, dst, sends, recv, to):
        return pltpu.make_async_remote_copy(
            src_ref=src, dst_ref=dst, send_sem=send_sem.at[sends], recv_sem=recv, device_id=to, device_id_type=MESH
        )

    def send(src, dst, sends, recv, to):
        remote(src, dst, sends, recv, to).start()

    def landed(region, recv):
        pltpu.make_async_copy(region, region, recv).wait()

    def out(src, dst, at):
        pltpu.make_async_copy(src, dst, out_sem.at[at]).start()

    w_load = pltpu.make_async_copy(w_hbm, wg.at[pl.ds(((core * NX + a) * NX + b) * 6, 6)], load_sem.at[2])
    cot_load = pltpu.make_async_copy(cot_hbm, cot, load_sem.at[3])

    def tok_load(h):
        for i in range(FB):
            pltpu.make_async_copy(
                tok_hbm.at[pl.ds(h * T, T), pl.ds(i * BLK, BLK)], toks[h].at[c * FB + i], load_sem.at[h]
            ).start()

    def tok_wait(h):
        region = toks[h].at[pl.ds(c * FB, FB)]
        pltpu.make_async_copy(region, region, load_sem.at[h]).wait()

    barrier = pltpu.get_barrier_semaphore()
    for to in (*z_to, *a_to, *b_to, sibling):
        pl.semaphore_signal(barrier, inc=1, device_id=to, device_id_type=MESH)
    tok_load(0)
    w_load.start()
    pltpu.make_async_copy(cols_hbm, cols, load_sem.at[4]).start()
    pltpu.make_async_copy(cols_hbm, cols_v, load_sem.at[5]).start()
    pl.semaphore_wait(barrier, 7)

    def ag_region(h, shard, way, step, p):
        rows = pl.ds(0, T) if step < 4 else pl.ds(way * HALF, HALF)
        return toks[h].at[pl.ds(shard * FB + p * (FB // NP), FB // NP), rows]

    def ag_send(h, way, step, p):
        shard = ring(c, (1 - step) if way == 0 else (step - 1), NZ)
        region = ag_region(h, shard, way, step, p)
        send(region, region, h, ag_sem.at[h, step - 1, p], z_to[way])

    def ag_event(h, step, p):
        n = FB // NP if step == 4 else 2 * FB // NP
        landed(toks[h].at[pl.ds(0, n)], ag_sem.at[h, step - 1, p])
        if step < 4:
            for way in range(2):
                ag_send(h, way, step + 1, p)

    def ag_open(h):
        for p in range(NP):
            for way in range(2):
                ag_send(h, way, 1, p)

    def w_region(core_, a_, b_, lo=0, n=6):
        return wg.at[pl.ds(((core_ * NX + a_) * NX + b_) * 6 + lo, n)]

    def b_of(q):
        return ring(b, (0, 1, -1, 2)[q], NX)

    def w_to_a(q):
        region = w_region(core, a, b_of(q))
        for way in range(2):
            send(region, region, 4, wa_sem.at[way, q], a_to[way])

    def w_to_sibling(g, q):
        region = w_region(core, ring(a, (0, 1, -1, 2)[g], NX), b_of(q))
        send(region, region, 4, wc_sem.at[0], sibling)

    def w_open():
        region = w_region(core, a, b)
        for way in range(2):
            send(region, region, 4, wb_sem.at[way], b_to[way])
        w_to_a(0)
        w_to_sibling(0, 0)

    def w_near_b():
        for way in range(2):
            q = 2 if way == 0 else 1
            landed(w_region(core, a, b_of(q)), wb_sem.at[way])
            region = w_region(core, a, b_of(q), 3 * way, 3)
            send(region, region, 4, wb_sem.at[2], b_to[way])
            w_to_a(q)
            w_to_sibling(0, q)

    def w_far_b():
        landed(w_region(core, a, b_of(3)), wb_sem.at[2])
        w_to_a(3)
        w_to_sibling(0, 3)

    def w_near_a(q):
        for way in range(2):
            g = 2 if way == 0 else 1
            a_ = ring(a, -1 if way == 0 else 1, NX)
            landed(w_region(core, a_, b_of(q)), wa_sem.at[way, q])
            region = w_region(core, a_, b_of(q), 3 * way, 3)
            send(region, region, 4, wa_sem.at[2, q], a_to[way])
            w_to_sibling(g, q)

    def w_far_a(q):
        landed(w_region(core, ring(a, 2, NX), b_of(q)), wa_sem.at[2, q])
        w_to_sibling(3, q)

    def w_close():
        landed(wg.at[pl.ds((1 - core) * DB, DB)], wc_sem.at[0])

    def plan_places():
        pltpu.make_async_copy(cols_hbm, cols, load_sem.at[4]).wait()
        pltpu.make_async_copy(cols_hbm, cols_v, load_sem.at[5]).wait()
        mine = cols_v[...]
        order = lax.broadcasted_iota(jnp.int32, (KP, DB), 0) * DB + lax.broadcasted_iota(jnp.int32, (KP, DB), 1)
        lane = lax.broadcasted_iota(jnp.int32, (8, BLK), 1)

        def body(k, carry):
            at, counts = carry
            for s in range(KP):
                col = cols[s, k]
                before = (col < mine) | ((col == mine) & (s * DB + k < order))
                at = at + jnp.where(before, 1, 0)
                counts = counts + jnp.where(lane == col, 1, 0)
            return at, counts

        at, counts = lax.fori_loop(
            0, DB, body, (jnp.zeros((KP, DB), jnp.int32), jnp.zeros((8, BLK), jnp.int32)), unroll=4
        )
        count_v[...] = counts
        copy = pltpu.make_async_copy(count_v, count, load_sem.at[6])
        copy.start()
        copy.wait()
        pair = lane
        keep = jnp.ones((8, BLK), jnp.int32)
        last = jnp.full((8, BLK), -1, jnp.int32)
        base = jnp.int32(0)
        for j in range(PB):
            n = count[0, j]
            pairs = lax.shift_right_logical(n + 1, 1)
            at = at + jnp.where(mine > j, n & 1, 0)
            keep = jnp.where(pair == base, 0, keep)
            last = last + jnp.where(lane >= j, pairs, 0)
            base = base + pairs
        place_v[...] = at
        copy = pltpu.make_async_copy(place_v, place, load_sem.at[6])
        copy.start()
        copy.wait()
        tab_v[pl.ds(8, 8)] = keep
        tab_v[pl.ds(16, 8)] = last

    def plan_table():
        slot = 2 * lax.broadcasted_iota(jnp.int32, (8, BLK), 1) + lax.broadcasted_iota(jnp.int32, (8, BLK), 0)

        def body(k, carry):
            rows, where = carry
            first = weight_position(k)
            for s in range(KP):
                hit = slot == place[s, k]
                rows = jnp.where(hit, k, rows)
                where = jnp.where(hit, first + s, where)
            return rows, where

        rows, where = lax.fori_loop(
            0, DB, body, (jnp.zeros((8, BLK), jnp.int32), jnp.full((8, BLK), ENT, jnp.int32)), unroll=2
        )
        tab_v[pl.ds(0, 8)] = rows
        tab_v[pl.ds(24, 8)] = where
        copy = pltpu.make_async_copy(tab_v, tab, load_sem.at[6])
        copy.start()
        copy.wait()

    def lanes(k):
        return pl.ds(pl.multiple_of(k * BLK, BLK), BLK)

    def fwd(h, lo, hi):
        tok = toks[h]

        def body(i, acc):
            xs = jnp.concatenate([tok[tab[TAB_K + s, i]] for s in range(2)], axis=1)
            ws = jnp.concatenate([wg[tab[TAB_W + s, i]] for s in range(2)], axis=0)
            acc = acc * tab[TAB_KEEP, i].astype(F32) + jnp.dot(xs, ws, preferred_element_type=F32)
            seg[i] = acc
            return acc

        start = jnp.zeros((T, BLK), F32) if lo == 0 else seg[lo - 1]
        lax.fori_loop(lo, hi, body, start, unroll=3)

    def gelu(h):
        rows = pl.ds(h * T, T)

        def body(j, carry):
            v = seg[tab[TAB_LAST, j]]
            k0 = 0.7978845608028654
            v2 = v * v
            th = jnp.tanh(k0 * (v + 0.044715 * (v2 * v)))
            half = 0.5 * (1.0 + th)
            slope = half + (0.5 * v) * (1.0 - th * th) * (k0 * (1.0 + 3 * 0.044715 * v2))
            act[rows, lanes(j)] = (v * half).astype(BF16)
            gps[h][j] = (cot[rows, lanes(j)].astype(F32) * slope).astype(BF16)
            return carry

        lax.fori_loop(0, PB, body, 0)

    def grad_x(h, shard):
        gp, dx = gps[h], dxs[h]

        def body(i, carry):
            k = shard * FB + i
            at = weight_position(k)
            gs = jnp.concatenate([gp[cols[s, k]] for s in range(2)], axis=1)
            ws = jnp.concatenate([wg[at + s] for s in range(2)], axis=1)
            out = lax.dot_general(gs, ws, (((1,), (1,)), ((), ())), preferred_element_type=F32)
            dx[:, lanes(k)] = out.astype(BF16)
            return carry

        lax.fori_loop(0, FB, body, 0, unroll=3)

    def grad_w(core_, a_):
        def body(i, carry):
            b_, j = i // 3, i % 3
            at = (((core_ * NX + a_) * NX + b_) * 3 + j) * 2
            x_ = a_ + (b_ - a_) * core_
            y_ = b_ + (a_ - b_) * core_
            k = ((y_ * NX + x_) * 2 + core_) * 3 + j
            xs = jnp.concatenate([tok[k] for tok in toks], axis=0)
            picks = [cols[s, k] for s in range(2)]
            gs = jnp.concatenate(
                [jnp.concatenate([gp[col] for gp in gps], axis=0) for col in picks], axis=1
            )
            out = lax.dot_general(xs, gs, (((0,), (0,)), ((), ())), preferred_element_type=F32)
            dw[at] = out[:, :BLK].astype(BF16)
            dw[at + 1] = out[:, BLK:].astype(BF16)
            return carry

        lax.fori_loop(0, 12, body, 0, unroll=2)

    def rs_rows(way, step):
        return pl.ds(0, HALF) if step == 1 else pl.ds(HALF + (step - 2) * T, T)

    def rs_send(h, way, step, p):
        shard = ring(c, (5 - step) if way == 0 else (step - 5), NZ)
        col = pl.ds(pl.multiple_of(shard * FEAT + p * PW, PW), PW)
        rows = pl.ds(way * HALF, HALF) if step == 1 else pl.ds(0, T)
        send(
            dxs[h].at[rows, col],
            rss[h].at[way, rs_rows(way, step), pl.ds(p * PW, PW)],
            2 + h,
            rs_sem.at[h, step - 1, p],
            z_to[way],
        )

    def rs_open(h):
        for p in range(NP):
            for way in range(2):
                rs_send(h, way, 1, p)

    def rs_wait(h, step, p):
        landed(rss[h].at[:, rs_rows(0, step), pl.ds(p * PW, PW)], rs_sem.at[h, step - 1, p])

    def rs_event(h, step, p):
        dx, rs = dxs[h], rss[h]
        rs_wait(h, step, p)
        if step < 4:
            for way in range(2):
                shard = ring(c, (4 - step) if way == 0 else (step - 4), NZ)
                rows = pl.ds(way * HALF, HALF) if step == 1 else pl.ds(0, T)

                def body(i, carry):
                    at = lanes(shard * FB + p * (PW // BLK) + i)
                    got = rs[way, rs_rows(way, step), lanes(p * (PW // BLK) + i)]
                    dx[rows, at] = (dx[rows, at].astype(F32) + got.astype(F32)).astype(BF16)
                    return carry

                lax.fori_loop(0, PW // BLK, body, 0, unroll=True)
                rs_send(h, way, step + 1, p)
        else:
            def body(i, carry):
                at = lanes(c * FB + p * (PW // BLK) + i)
                total = dx[:, at].astype(F32)
                for way in range(2):
                    total += rs[way, rs_rows(way, 4), lanes(p * (PW // BLK) + i)].astype(F32)
                gt[pl.ds(h * T, T), lanes(p * (PW // BLK) + i)] = total.astype(BF16)
                return carry

            lax.fori_loop(0, PW // BLK, body, 0, unroll=True)

    def w_at(a_, b_=0):
        return ((core * NX + a_) * NX + b_) * 6

    def pair_send(a_):
        src = dw.at[pl.ds((((1 - core) * NX + a_) * NX) * 6, 24)]
        send(src, pr.at[pl.ds(a_ * 24, 24)], 5, gc_sem.at[a_], sibling)

    def add_blocks(dst, n, *srcs):
        def body(i, carry):
            total = dw[dst + i].astype(F32)
            for ref, at in srcs:
                total += ref[at + i].astype(F32)
            dw[dst + i] = total.astype(BF16)
            return carry

        lax.fori_loop(0, n, body, 0, unroll=2)

    def pair_add(a_):
        landed(pr.at[pl.ds(a_ * 24, 24)], gc_sem.at[a_])
        add_blocks(w_at(a_), 24, (pr, a_ * 24))

    def part(buf, way, step, size):
        off = way * (size + size // 2) + (0 if step == 0 else size // 2)
        return buf.at[pl.ds(off, size // 2 if step == 0 else size)], off

    def ring_open(buf, far, size, sems, tos):
        for way in range(2):
            dst, _ = part(buf, way, 0, size)
            send(dw.at[pl.ds(far + way * (size // 2), size // 2)], dst, 5, sems.at[way, 0], tos[way])

    def ring_middle(buf, nexts, size, sems, tos):
        for way in range(2):
            got, off = part(buf, way, 0, size)
            landed(got, sems.at[way, 0])
            add_blocks(nexts[way] + way * (size // 2), size // 2, (buf, off))
            dst, _ = part(buf, way, 1, size)
            send(dw.at[pl.ds(nexts[way], size)], dst, 5, sems.at[way, 1], tos[way])

    def ring_close(buf, own, size, sems, tos):
        srcs = []
        for way in range(2):
            got, off = part(buf, way, 1, size)
            landed(got, sems.at[way, 1])
            srcs.append((buf, off))
        add_blocks(own, size, *srcs)

    a_near = (w_at(ring(a, 1, NX)), w_at(ring(a, -1, NX)))
    b_near = (w_at(a, ring(b, 1, NX)), w_at(a, ring(b, -1, NX)))

    wg[ENT] = jnp.zeros((BLK, BLK), BF16)
    tok_wait(0)
    ag_open(0)
    w_load.wait()
    w_open()
    tok_load(1)
    cot_load.start()
    ag_event(0, 1, 0)
    w_near_b()
    w_near_a(0)
    ag_event(0, 1, 1)
    w_far_b()
    ag_event(0, 2, 0)
    w_near_a(1)
    w_near_a(2)
    ag_event(0, 2, 1)
    w_near_a(3)
    w_far_a(0)
    ag_event(0, 3, 0)
    w_far_a(1)
    w_far_a(2)
    w_far_a(3)
    tok_wait(1)
    ag_event(0, 3, 1)
    ag_open(1)
    plan_places()
    plan_table()
    cot_load.wait()
    w_close()
    ag_event(0, 4, 0)
    ag_event(0, 4, 1)

    quarter = PAIRS // 4
    fwd(0, 0, quarter)
    ag_event(1, 1, 0)
    fwd(0, quarter, 2 * quarter)
    ag_event(1, 1, 1)
    fwd(0, 2 * quarter, 3 * quarter)
    fwd(0, 3 * quarter, PAIRS)
    ag_event(1, 2, 0)
    gelu(0)
    grad_x(0, ring(c, 4, NZ))
    ag_event(1, 2, 1)
    grad_x(0, ring(c, 3, NZ))
    grad_x(0, ring(c, -3, NZ))
    grad_x(0, ring(c, 2, NZ))
    ag_event(1, 3, 0)
    grad_x(0, ring(c, -2, NZ))
    grad_x(0, ring(c, 1, NZ))
    grad_x(0, ring(c, -1, NZ))
    grad_x(0, c)
    ag_event(1, 3, 1)
    rs_open(0)
    ag_event(1, 4, 0)
    ag_event(1, 4, 1)

    fwd(1, 0, quarter)
    rs_event(0, 1, 0)
    fwd(1, quarter, 2 * quarter)
    rs_event(0, 1, 1)
    fwd(1, 2 * quarter, 3 * quarter)
    fwd(1, 3 * quarter, PAIRS)
    gelu(1)
    rs_event(0, 2, 0)
    for g in range(2):
        grad_w(1 - core, g)
        pair_send(g)
    rs_event(0, 2, 1)
    for g in range(2, 4):
        grad_w(1 - core, g)
        pair_send(g)
    grad_w(core, ring(a, 2, NX))
    rs_event(0, 3, 0)
    grad_x(1, ring(c, 4, NZ))
    rs_open(1)
    pair_add(ring(a, 2, NX))
    ring_open(bufa, w_at(ring(a, 2, NX)), 24, ga_sem, a_to)
    grad_w(core, ring(a, 1, NX))
    grad_w(core, ring(a, -1, NX))
    rs_event(0, 3, 1)
    grad_x(1, ring(c, 3, NZ))
    grad_x(1, ring(c, -3, NZ))
    pair_add(ring(a, 1, NX))
    pair_add(ring(a, -1, NX))
    ring_middle(bufa, a_near, 24, ga_sem, a_to)
    rs_event(1, 1, 0)
    grad_w(core, a)
    pair_add(a)
    rs_event(0, 4, 0)
    grad_x(1, ring(c, 2, NZ))
    grad_x(1, ring(c, -2, NZ))
    rs_event(1, 1, 1)
    rs_event(0, 4, 1)
    grad_x(1, ring(c, 1, NZ))
    grad_x(1, ring(c, -1, NZ))
    grad_x(1, c)
    rs_event(1, 2, 0)
    ring_close(bufa, w_at(a), 24, ga_sem, a_to)
    ring_open(bufb, w_at(a, ring(b, 2, NX)), 6, gb_sem, b_to)
    rs_event(1, 2, 1)
    ring_middle(bufb, b_near, 6, gb_sem, b_to)
    rs_event(1, 3, 0)
    ring_close(bufb, w_at(a, b), 6, gb_sem, b_to)
    out(dw.at[pl.ds(w_at(a, b), 6)], gb, 0)
    rs_event(1, 3, 1)
    for h in range(CHUNKS):
        landed(toks[h].at[pl.ds(0, 7 * FB)], send_sem.at[h])
    landed(dx0.at[:, pl.ds(0, 7 * FEAT)], send_sem.at[2])
    landed(wg.at[pl.ds(0, 31 * 6)], send_sem.at[4])
    landed(dw.at[pl.ds(0, 31 * 6)], send_sem.at[5])
    pltpu.make_async_copy(dw.at[pl.ds(0, 6)], gb, out_sem.at[0]).wait()
    rs_event(1, 4, 0)
    rs_event(1, 4, 1)

    landed(dx1.at[:, pl.ds(0, 7 * FEAT)], send_sem.at[3])


def finish(act, gt, gb, act_out, gt_out, gb_out, sem_out):
    parts = [(act, act_out, pl.ds(i * 64, 64)) for i in range(4)]
    parts += [(gt, gt_out, pl.ds(i * 128, 128)) for i in range(2)]
    parts += [(gb, gb_out, pl.ds(0, 6))]
    stores = [pltpu.make_async_copy(mid.at[at], dst.at[at], sem_out.at[i]) for i, (mid, dst, at) in enumerate(parts)]
    for copy in stores:
        copy.start()
    for copy in stores:
        copy.wait()


def on_device(tokens, weight_blocks, block_cols, cotangent):
    hbm = pl.BlockSpec(memory_space=pltpu.HBM)
    arrays = (block_cols.T, tokens, weight_blocks.reshape(6, BLK, BLK), cotangent)
    in_hbm = [pltpu.with_memory_space_constraint(v, pltpu.HBM) for v in arrays]
    dma = pltpu.SemaphoreType.DMA
    act, grad_tokens, grad_blocks = pl.pallas_call(
        kernel,
        out_shape=(
            jax.ShapeDtypeStruct((CHUNKS * T, PB * BLK), BF16),
            jax.ShapeDtypeStruct((CHUNKS * T, FEAT), BF16),
            jax.ShapeDtypeStruct((6, BLK, BLK), BF16),
        ),
        in_specs=[hbm] * 4,
        out_specs=(pl.BlockSpec(memory_space=pltpu.VMEM),) * 3,
        scratch_shapes=[
            pltpu.VMEM((DB, T, BLK), BF16),
            pltpu.VMEM((DB, T, BLK), BF16),
            pltpu.VMEM((ENT + 1, BLK, BLK), BF16),
            pltpu.VMEM((PAIRS, T, BLK), F32),
            pltpu.VMEM((CHUNKS * T, PB * BLK), BF16),
            pltpu.VMEM((PB, T, BLK), BF16),
            pltpu.VMEM((PB, T, BLK), BF16),
            pltpu.VMEM((T, DB * BLK), BF16),
            pltpu.VMEM((T, DB * BLK), BF16),
            pltpu.VMEM((2, HALF + 3 * T, FEAT), BF16),
            pltpu.VMEM((2, HALF + 3 * T, FEAT), BF16),
            pltpu.VMEM((ENT, BLK, BLK), BF16),
            pltpu.VMEM((ENT // 2, BLK, BLK), BF16),
            pltpu.VMEM((2 * 36, BLK, BLK), BF16),
            pltpu.VMEM((2 * 9, BLK, BLK), BF16),
            pltpu.VMEM((KP, DB), jnp.int32),
            pltpu.SMEM((KP, DB), jnp.int32),
            pltpu.VMEM((8, BLK), jnp.int32),
            pltpu.SMEM((8, BLK), jnp.int32),
            pltpu.VMEM((KP, DB), jnp.int32),
            pltpu.SMEM((KP, DB), jnp.int32),
            pltpu.VMEM((32, BLK), jnp.int32),
            pltpu.SMEM((32, BLK), jnp.int32),
            dma((7,)),
            dma((1,)),
            dma((6,)),
            dma((CHUNKS, 4, NP)),
            dma((CHUNKS, 4, NP)),
            dma((3,)),
            dma((3, 4)),
            dma((1,)),
            dma((4,)),
            dma((2, 2)),
            dma((2, 2)),
        ],
        compiler_params=pltpu.CompilerParams(
            collective_id=0, has_side_effects=True, vmem_limit_bytes=50 * 1024 * 1024
        ),
        cost_estimate=pl.CostEstimate(flops=4_831_838_208, bytes_accessed=6_000_000, transcendentals=786_432),
    )(*in_hbm)
    act, grad_tokens, grad_blocks = pl.pallas_call(
        finish,
        out_shape=tuple(jax.ShapeDtypeStruct(v.shape, v.dtype) for v in (act, grad_tokens, grad_blocks)),
        in_specs=[pl.BlockSpec(memory_space=pltpu.VMEM)] * 3,
        out_specs=(hbm,) * 3,
        scratch_shapes=[dma((7,))],
        compiler_params=pltpu.CompilerParams(vmem_limit_bytes=4 * 1024 * 1024),
    )(act, grad_tokens, grad_blocks)
    return act, grad_tokens, grad_blocks.reshape(3, KP, BLK, BLK)


def solution(mesh):
    return jax.shard_map(
        on_device,
        mesh=mesh,
        in_specs=(P("row", "col"), P("row", "col", None, None), P(None, "col"), P("row", "col")),
        out_specs=(P("row", "col"), P("row", "col"), P("row", "col", None, None)),
        check_vma=False,
    )
```
